128 devices in a mesh: pgrp: 4 (over y_lo, core), srow: 32 (over x, z, y_hi).
Axes of the slice: x: 4, y: 4 (y_hi: 2, y_lo: 2; y = y_hi * 2 + y_lo), z: 4, core: 2. Of those that a mesh axis runs over, the one named last changes fastest.
Arguments:
- kernel: bfloat16 [608, 224, 512], P('srow', None, 'pgrp'), may hold values from -0.0234375 to 0.0234375
- probes: bfloat16 [4, 608, 224], P(None, 'srow', 'pgrp'), may hold values from -6 to 6
- prior_var: float32 [512], P('pgrp'), may hold values from 0.3 to 3
- noise_var: float32 [608], P('srow'), may hold values from 0.1 to 1
Outputs:
- hessian_probes: float32 [4, 608, 224], P(None, 'srow', 'pgrp')
The draws below stay inside these ranges and needn't reach their ends.
All inputs are finite; a program needn't handle non-finite values.
Results may differ from the reference program's by a relative error of at most 0.0022.
Values may be sent and summed in bfloat16 or wider, within the bound.
A program may use at most 64 MiB of HBM per device.

```python
import math
import jax
import jax.numpy as jnp
from jax import lax

NS = 608
NP = 512
NT = 224
NV = 4
N_SROW = 32


def block_scale(key, extent, cuts, least, high):
    gain = 1.0
    for axis_at, parts in cuts:
        heights = jax.random.uniform(jax.random.fold_in(jax.random.fold_in(key, 6), axis_at), (parts,), jnp.float32, least / len(cuts), high / len(cuts))
        gain = gain * jnp.repeat(jnp.exp(heights), extent[axis_at] // parts).reshape((-1,) + (1,) * (len(extent) - 1 - axis_at))
    return gain


def gaussian(key, dims, width, reach, shards=(), held_as=jnp.bfloat16):
    result = jax.random.normal(key, dims, jnp.float32) * width
    if len(shards) > 0:
        result = block_scale(key, dims, shards, -0.22, 0.18) * result
    return jnp.clip(result, min=-reach, max=reach).astype(held_as)


def setup_inputs(seed: int = 0) -> dict:
    arg_keys = jax.random.split(jax.random.key(seed), 5)
    return {
        "kernel": gaussian(arg_keys[0], (NS, NT, NP), (NT * (NS + NP) // 4) ** -0.5, 0.0234375, ((0, 32), (2, 4))),
        "probes": gaussian(arg_keys[1], (NV, NS, NT), 1.0, 6.0, ((1, 32), (2, 4))),
        "prior_var": jnp.clip(jnp.exp(math.log(3.0) - 2.3025851 * jax.random.uniform(arg_keys[2], (NP,), jnp.float32) ** block_scale(arg_keys[2], (NP,), ((0, 4),), -0.2, 0.2)), 0.3, 3.0),
        "noise_var": jnp.clip(jnp.exp(math.log(1.0) - 2.3025851 * jax.random.uniform(arg_keys[3], (NS,), jnp.float32) ** block_scale(arg_keys[3], (NS,), ((0, 32),), -0.2, 0.2)), 0.1, 1.0),
    }


def reference(kernel, probes, prior_var, noise_var):
    length = kernel.shape[1]
    padded_len = 2 * length
    per_block = NS // N_SROW
    probe_freq = jnp.fft.rfft(probes.astype(jnp.float32), n=padded_len, axis=2)
    freqs = probe_freq.shape[2]
    kernel_blocks = kernel.reshape(N_SROW, per_block, length, NP)
    probe_blocks = probe_freq.reshape(NV, N_SROW, per_block, freqs).transpose(1, 0, 2, 3)

    def adjoint_step(accum, pieces):
        kernel_piece, probe_piece = pieces
        kernel_freq = jnp.fft.rfft(kernel_piece.astype(jnp.float32), n=padded_len, axis=1)
        return accum + jnp.einsum('sfp,nsf->npf', jnp.conj(kernel_freq), probe_piece), None

    start = jnp.zeros((NV, NP, freqs), probe_freq.dtype)
    accum, unused = lax.scan(adjoint_step, start, (kernel_blocks, probe_blocks))
    adjoint = jnp.fft.irfft(accum, n=padded_len, axis=2)[:, :, :length]
    params = (adjoint * prior_var[None, :, None]).astype(jnp.bfloat16)
    param_freq = jnp.fft.rfft(params.astype(jnp.float32), n=padded_len, axis=2)

    def forward_step(kernel_piece):
        kernel_freq = jnp.fft.rfft(kernel_piece.astype(jnp.float32), n=padded_len, axis=1)
        product = jnp.einsum('sfp,npf->nsf', kernel_freq, param_freq)
        return jnp.fft.irfft(product, n=padded_len, axis=2)[:, :, :length]

    pieces = lax.map(forward_step, kernel_blocks)
    forward = pieces.transpose(1, 0, 2, 3).reshape(NV, NS, length)
    return forward + noise_var[None, :, None] * probes.astype(jnp.float32)
```

```python
import functools

import jax
import jax.numpy as jnp
from jax import lax
from jax.experimental import pallas as pl
from jax.experimental.pallas import tpu as pltpu
from jax.sharding import PartitionSpec as P

MESH = pl.DeviceIdType.MESH
F32 = jnp.float32
BF16 = jnp.bfloat16

NV, NS, NT, NP = 4, 19, 224, 128
NQ, NR = 4, 32
STEP = 32
NH = NT // STEP
PAIRS = (NH + 1) // 2
ROWS = NV * STEP
WIDE = 256
LEAD = NT - STEP
TALL = LEAD + WIDE
PART = NT // NQ
HALF = 64
SROWS = 24
PROWS = 2 * SROWS


def owner_of(h, n):
    return 8 * n + 2 * ((n + h // 2) % 4) + h % 2


def block_of(r):
    n = r // 8
    h = 2 * lax.rem(lax.rem(r // 2, 4) - n + 4, 4) + lax.rem(r, 2)
    return h, n


def kernel_body(
    probes_ref, prior_ref, noise_ref, k_hbm, out_ref,
    kpad, base, y_ref, pf, psend, precv, rsend, rrecv, xall, f_ref, fsend, frecv,
    k_sem, ps_sem, pr_sem, rs_sem, rr_sem, xs_sem, xr_sem, fs_sem, fr_sem,
):
    me = lax.axis_index("srow")
    grp = lax.axis_index("pgrp")
    my_h, my_n = block_of(me)
    mine = my_h * NV + my_n
    owns = my_h < NH

    barrier = pltpu.get_barrier_semaphore()

    def greet(d, _):
        pl.semaphore_signal(
            barrier, inc=1, device_id={"srow": lax.rem(me + d, NR)}, device_id_type=MESH
        )
        return 0

    for d in range(1, NQ):
        pl.semaphore_signal(
            barrier, inc=1, device_id={"pgrp": lax.rem(grp + d, NQ)}, device_id_type=MESH
        )
    lax.fori_loop(1, NR, greet, 0)

    k_copy = pltpu.make_async_copy(k_hbm, kpad.at[:, pl.ds(LEAD, NT), :], k_sem)
    k_copy.start()

    pf[...] = jnp.zeros_like(pf)
    for n in range(NV):
        row, lane = (n % 2) * SROWS, (n // 2) * HALF
        pf[row : row + NS, lane : lane + PART] = probes_ref[n].astype(F32)
    psend[...] = pf[...].astype(BF16)
    kpad[:, 0:LEAD, :] = jnp.zeros((NS, LEAD, NP), BF16)
    kpad[:, LEAD + NT : TALL, :] = jnp.zeros((NS, TALL - LEAD - NT, NP), BF16)
    f_ref[...] = jnp.zeros_like(f_ref)

    pl.semaphore_wait(barrier, NQ - 1 + NR - 1)

    def probe_copy(d):
        to = lax.rem(grp + d, NQ)
        return pltpu.make_async_remote_copy(
            src_ref=psend, dst_ref=precv.at[d - 1], send_sem=ps_sem.at[d - 1],
            recv_sem=pr_sem.at[d - 1], device_id={"pgrp": to}, device_id_type=MESH,
        )

    for d in range(1, NQ):
        probe_copy(d).start()
    lanes = lax.broadcasted_iota(jnp.int32, (SROWS, NP), 1)
    zeros = jnp.zeros((SROWS, WIDE - NP), F32)

    def place(part, group):
        for n in range(NV):
            row, lane = (n % 2) * SROWS, (n // 2) * HALF
            inside = (lanes >= lane) & (lanes < lane + PART)
            piece = jnp.where(inside, part[row : row + SROWS, :].astype(F32), 0.0)
            wide = jnp.concatenate([piece, zeros], axis=1)
            shift = lax.rem(group * PART + (WIDE - (STEP - 1) - lane), WIDE)
            y_ref[n] += pltpu.roll(wide, shift, 1)

    y_ref[...] = jnp.zeros_like(y_ref)
    place(psend, grp)
    for d in range(1, NQ):
        probe_copy(d).wait_recv()
        place(precv[d - 1], lax.rem(grp + NQ - d, NQ))

    inside_wide = lax.broadcasted_iota(jnp.int32, (STEP, WIDE), 1) < NT

    def make_base(s, _):
        for n in range(NV):
            line = jnp.broadcast_to(y_ref[n, pl.ds(s, 1), :], (STEP, WIDE))
            turned = pltpu.roll(line, 0, 1, stride=1, stride_axis=0)
            turned = jnp.where(inside_wide, turned, 0.0)
            base[s, n * STEP : (n + 1) * STEP, :] = turned.astype(BF16)
        return 0

    lax.fori_loop(0, NS, make_base, 0)
    k_copy.wait()

    def share_copy(h, n, slot):
        return pltpu.make_async_remote_copy(
            src_ref=rsend.at[h * NV + n], dst_ref=rrecv.at[slot], send_sem=rs_sem.at[h * NV + n],
            recv_sem=rr_sem.at[slot], device_id={"srow": owner_of(h, n)}, device_id_type=MESH,
        )

    def spans(hp):
        return [h for h in (2 * hp, 2 * hp + 1) if h < NH]

    for hp in range(PAIRS):
        hs = spans(hp)

        def add_sensor(s, acc):
            w = jnp.concatenate(
                [kpad[s, LEAD - STEP * h : LEAD - STEP * h + WIDE, :] for h in hs], axis=1
            )
            return acc + jnp.dot(base[s], w, preferred_element_type=F32)

        acc = lax.fori_loop(0, NS, add_sensor, jnp.zeros((ROWS, NP * len(hs)), F32))
        for j, h in enumerate(hs):
            for n in range(NV):
                rsend[h * NV + n] = acc[n * STEP : (n + 1) * STEP, j * NP : (j + 1) * NP]

        def send_share(j, _):
            j = lax.rem(j + me, NV * len(hs))
            n, h = lax.rem(j, NV), hs[0] + j // NV

            @pl.when(owner_of(h, n) != me)
            def _():
                share_copy(h, n, me).start()

            return 0

        lax.fori_loop(0, NV * len(hs), send_share, 0)

    def param_copy(d):
        to = lax.rem(me + d, NR)
        return pltpu.make_async_remote_copy(
            src_ref=xall.at[mine], dst_ref=xall.at[mine], send_sem=xs_sem.at[d],
            recv_sem=xr_sem.at[mine], device_id={"srow": to}, device_id_type=MESH,
        )

    @pl.when(owns)
    def _():
        def take(d, total):
            slot = lax.rem(me + d, NR)
            share_copy(my_h, my_n, slot).wait_recv()
            return total + rrecv[slot]

        total = lax.fori_loop(1, NR, take, rsend[mine])
        scaled = total * prior_ref[...]
        row = lax.broadcasted_iota(jnp.int32, (STEP, STEP), 0)
        col = lax.broadcasted_iota(jnp.int32, (STEP, STEP), 1)
        flip = (row + col == STEP - 1).astype(BF16)
        xall[mine] = jnp.dot(flip, scaled.astype(BF16), preferred_element_type=F32).astype(BF16)

        def send_params(d, _):
            param_copy(d).start()
            return 0

        lax.fori_loop(1, NR, send_params, 0)

    def wait_block(b, _):
        @pl.when(b != mine)
        def _():
            pltpu.make_async_remote_copy(
                src_ref=xall.at[b], dst_ref=xall.at[b], send_sem=xs_sem.at[0],
                recv_sem=xr_sem.at[b], device_id={"srow": me}, device_id_type=MESH,
            ).wait_recv()

        return 0

    lax.fori_loop(0, NH * NV, wait_block, 0)

    def x_of(h):
        return xall[h * NV : (h + 1) * NV].reshape(ROWS, NP)

    inside_rows = lax.broadcasted_iota(jnp.int32, (ROWS, WIDE), 1) < NT

    def forward_sensor(s, _):
        z = jnp.zeros((ROWS, WIDE), F32)
        for hp in range(PAIRS):
            hs = spans(hp)
            x = jnp.concatenate([x_of(h) for h in hs], axis=1)
            w = jnp.concatenate(
                [kpad[s, LEAD - STEP * h : LEAD - STEP * h + WIDE, :] for h in hs], axis=1
            )
            z = z + lax.dot_general(x, w, (((1,), (1,)), ((), ())), preferred_element_type=F32)
        z = jnp.where(inside_rows, z, 0.0)
        for n in range(NV):
            turned = pltpu.roll(z[n * STEP : (n + 1) * STEP, :], 0, 1, stride=1, stride_axis=0)
            f_ref[n, pl.ds(s, 1), :] = jnp.sum(turned, axis=0, keepdims=True)
        return 0

    lax.fori_loop(0, NS, forward_sensor, 0)

    first = lanes < HALF
    for q in range(NQ):
        for n in range(2):
            low = pltpu.roll(f_ref[n], (WIDE - PART * q) % WIDE, 1)[:, :NP]
            high = pltpu.roll(f_ref[n + 2], (WIDE - PART * q + HALF) % WIDE, 1)[:, :NP]
            fsend[q, n * SROWS : (n + 1) * SROWS, :] = jnp.where(first, low, high)

    def sum_copy(d):
        to = lax.rem(grp + d, NQ)
        return pltpu.make_async_remote_copy(
            src_ref=fsend.at[to], dst_ref=frecv.at[d - 1], send_sem=fs_sem.at[d - 1],
            recv_sem=fr_sem.at[d - 1], device_id={"pgrp": to}, device_id_type=MESH,
        )

    for d in range(1, NQ):
        sum_copy(d).start()
    eye = lax.broadcasted_iota(jnp.int32, (NS, NS), 0) == lax.broadcasted_iota(jnp.int32, (NS, NS), 1)
    noise = jnp.sum(jnp.where(eye, noise_ref[...], 0.0), axis=1, keepdims=True)
    total = fsend[grp]
    for d in range(1, NQ):
        sum_copy(d).wait_recv()
        total = total + frecv[d - 1]
    back = pltpu.roll(total, NP - HALF, 1)
    for n in range(NV):
        part = (total if n < 2 else back)[(n % 2) * SROWS : (n % 2) * SROWS + NS, :PART]
        out_ref[n] = part + noise * probes_ref[n].astype(F32)

    for d in range(1, NQ):
        probe_copy(d).wait_send()
        sum_copy(d).wait_send()

    def drain_share(b, _):
        n, h = lax.rem(b, NV), b // NV

        @pl.when(owner_of(h, n) != me)
        def _():
            share_copy(h, n, me).wait_send()

        return 0

    lax.fori_loop(0, NH * NV, drain_share, 0)

    @pl.when(owns)
    def _():
        def drain_params(d, _):
            param_copy(d).wait_send()
            return 0

        lax.fori_loop(1, NR, drain_params, 0)


def on_device(kernel, probes, prior_var, noise_var):
    vmem = pl.BlockSpec(memory_space=pltpu.VMEM)
    dma = pltpu.SemaphoreType.DMA
    return pl.pallas_call(
        kernel_body,
        out_shape=jax.ShapeDtypeStruct((NV, NS, PART), F32),
        in_specs=[vmem, vmem, vmem, pl.BlockSpec(memory_space=pl.ANY)],
        out_specs=vmem,
        scratch_shapes=[
            pltpu.VMEM((NS, TALL, NP), BF16),
            pltpu.VMEM((NS, ROWS, WIDE), BF16),
            pltpu.VMEM((NV, SROWS, WIDE), F32),
            pltpu.VMEM((PROWS, NP), F32),
            pltpu.VMEM((PROWS, NP), BF16),
            pltpu.VMEM((NQ - 1, PROWS, NP), BF16),
            pltpu.VMEM((NH * NV, STEP, NP), F32),
            pltpu.VMEM((NR, STEP, NP), F32),
            pltpu.VMEM((NH * NV, STEP, NP), BF16),
            pltpu.VMEM((NV, SROWS, WIDE), F32),
            pltpu.VMEM((NQ, PROWS, NP), F32),
            pltpu.VMEM((NQ - 1, PROWS, NP), F32),
            dma,
            dma((NQ - 1,)),
            dma((NQ - 1,)),
            dma((NH * NV,)),
            dma((NR,)),
            dma((NR,)),
            dma((NH * NV,)),
            dma((NQ - 1,)),
            dma((NQ - 1,)),
        ],
        compiler_params=pltpu.CompilerParams(
            collective_id=0, has_side_effects=True, vmem_limit_bytes=32 * 2**20
        ),
        cost_estimate=pl.CostEstimate(flops=2 * 10**9, bytes_accessed=2 * 10**6, transcendentals=0),
    )(probes, prior_var.reshape(1, NP), noise_var.reshape(1, NS), kernel)


def solution(mesh):
    placed = (P("srow", None, "pgrp"), P(None, "srow", "pgrp"), P("pgrp"), P("srow"))
    return jax.shard_map(
        on_device, mesh=mesh, in_specs=placed, out_specs=P(None, "srow", "pgrp"), check_vma=False
    )
```

```python
import functools

import jax
import jax.numpy as jnp
from jax import lax
from jax.experimental import pallas as pl
from jax.experimental.pallas import tpu as pltpu
from jax.sharding import PartitionSpec as P

MESH = pl.DeviceIdType.MESH
F32 = jnp.float32
BF16 = jnp.bfloat16

NV, NS, NT, NP = 4, 19, 224, 128
NQ, NR = 4, 32
STEP = 32
NH = NT // STEP
PAIRS = (NH + 1) // 2
ROWS = NV * STEP
WIDE = 256
LEAD = NT - STEP
TALL = LEAD + WIDE
PART = NT // NQ
HALF = 64
SPLIT = (NS + 1) // 2
SROWS = SPLIT * NV
PROWS = 48


def owner_of(h, n):
    return 8 * n + 2 * ((n + h // 2) % 4) + h % 2


def block_of(r):
    n = r // 8
    h = 2 * lax.rem(lax.rem(r // 2, 4) - n + 4, 4) + lax.rem(r, 2)
    return h, n


def kernel_body(
    probes_hbm, prior_hbm, noise_hbm, k_hbm, out_ref,
    probes_ref, prior_ref, noise_ref, kpad, base, y_ref, pf, psend, precv, rsend, rrecv, xall, f_ref, fsend, frecv,
    in_sem, ps_sem, pr_sem, rs_sem, rr_sem, xs_sem, xr_sem, fs_sem, fr_sem,
):
    me = lax.axis_index("srow")
    grp = lax.axis_index("pgrp")
    my_h, my_n = block_of(me)
    mine = my_h * NV + my_n
    owns = my_h < NH

    barrier = pltpu.get_barrier_semaphore()

    def greet(d, _):
        pl.semaphore_signal(
            barrier, inc=1, device_id={"srow": lax.rem(me + d, NR)}, device_id_type=MESH
        )
        return 0

    for d in range(1, NQ):
        pl.semaphore_signal(
            barrier, inc=1, device_id={"pgrp": lax.rem(grp + d, NQ)}, device_id_type=MESH
        )
    lax.fori_loop(1, NR, greet, 0)

    in_copies = [
        pltpu.make_async_copy(src, dst, in_sem.at[i])
        for i, (src, dst) in enumerate(
            (
                (probes_hbm, probes_ref),
                (k_hbm, kpad.at[:, pl.ds(LEAD, NT), :]),
                (prior_hbm, prior_ref),
                (noise_hbm, noise_ref),
            )
        )
    ]
    for copy in in_copies:
        copy.start()

    kpad[:, 0:LEAD, :] = jnp.zeros((NS, LEAD, NP), BF16)
    kpad[:, LEAD + NT : TALL, :] = jnp.zeros((NS, TALL - LEAD - NT, NP), BF16)
    f_ref[...] = jnp.zeros_like(f_ref)
    pf[...] = jnp.zeros_like(pf)
    in_copies[0].wait()
    for s in range(NS):
        row, lane = s % SPLIT * NV, s // SPLIT * HALF
        pf[row : row + NV, lane : lane + PART] = probes_ref[s].astype(F32)
    psend[...] = pf[...].astype(BF16)

    pl.semaphore_wait(barrier, NQ - 1 + NR - 1)

    def probe_copy(d):
        to = lax.rem(grp + d, NQ)
        return pltpu.make_async_remote_copy(
            src_ref=psend, dst_ref=precv.at[d - 1], send_sem=ps_sem.at[d - 1],
            recv_sem=pr_sem.at[d - 1], device_id={"pgrp": to}, device_id_type=MESH,
        )

    for d in range(1, NQ):
        probe_copy(d).start()
    lanes = lax.broadcasted_iota(jnp.int32, (SROWS, NP), 1)
    zeros = jnp.zeros((SROWS, WIDE - NP), F32)

    def place(part, group):
        part = part[:SROWS].astype(F32)
        for half in range(2):
            lane = half * HALF
            inside = (lanes >= lane) & (lanes < lane + PART)
            wide = jnp.concatenate([jnp.where(inside, part, 0.0), zeros], axis=1)
            shift = lax.rem(group * PART + (WIDE - (STEP - 1) - lane), WIDE)
            y_ref[half * SROWS : (half + 1) * SROWS, :] += pltpu.roll(wide, shift, 1)

    y_ref[...] = jnp.zeros_like(y_ref)
    place(psend, grp)
    for d in range(1, NQ):
        probe_copy(d).wait_recv()
        place(precv[d - 1], lax.rem(grp + NQ - d, NQ))

    inside_wide = lax.broadcasted_iota(jnp.int32, (STEP, WIDE), 1) < NT

    for s in range(NS):
        for n in range(NV):
            line = jnp.broadcast_to(y_ref[s * NV + n : s * NV + n + 1, :], (STEP, WIDE))
            turned = pltpu.roll(line, 0, 1, stride=1, stride_axis=0)
            turned = jnp.where(inside_wide, turned, 0.0)
            base[s, n * STEP : (n + 1) * STEP, :] = turned.astype(BF16)
    in_copies[1].wait()

    def share_copy(h, n, slot):
        return pltpu.make_async_remote_copy(
            src_ref=rsend.at[h * NV + n], dst_ref=rrecv.at[slot], send_sem=rs_sem.at[h * NV + n],
            recv_sem=rr_sem.at[slot], device_id={"srow": owner_of(h, n)}, device_id_type=MESH,
        )

    def spans(hp):
        return [h for h in (2 * hp, 2 * hp + 1) if h < NH]

    for hp in range(PAIRS):
        hs = spans(hp)

        low = STEP * hs[0] // NP * NP
        x = jnp.concatenate([base[s, :, low:] for s in range(NS)], axis=1)
        w = jnp.concatenate(
            [
                kpad[:, LEAD - STEP * h + low : LEAD - STEP * h + WIDE, :].reshape(-1, NP)
                for h in hs
            ],
            axis=1,
        )
        acc = jnp.dot(x, w, preferred_element_type=F32)
        for j, h in enumerate(hs):
            for n in range(NV):
                rsend[h * NV + n] = acc[n * STEP : (n + 1) * STEP, j * NP : (j + 1) * NP]

        def send_share(j, _):
            j = lax.rem(j + me, NV * len(hs))
            n, h = lax.rem(j, NV), hs[0] + j // NV

            @pl.when(owner_of(h, n) != me)
            def _():
                share_copy(h, n, me).start()

            return 0

        lax.fori_loop(0, NV * len(hs), send_share, 0)

    def param_copy(d):
        to = lax.rem(me + d, NR)
        return pltpu.make_async_remote_copy(
            src_ref=xall.at[mine], dst_ref=xall.at[mine], send_sem=xs_sem.at[d],
            recv_sem=xr_sem.at[mine], device_id={"srow": to}, device_id_type=MESH,
        )

    in_copies[2].wait()
    in_copies[3].wait()

    @pl.when(owns)
    def _():
        def take(d, total):
            slot = lax.rem(me + d, NR)
            share_copy(my_h, my_n, slot).wait_recv()
            return total + rrecv[slot]

        total = lax.fori_loop(1, NR, take, rsend[mine])
        scaled = total * prior_ref[...]
        row = lax.broadcasted_iota(jnp.int32, (STEP, STEP), 0)
        col = lax.broadcasted_iota(jnp.int32, (STEP, STEP), 1)
        flip = (row + col == STEP - 1).astype(BF16)
        xall[mine] = jnp.dot(flip, scaled.astype(BF16), preferred_element_type=F32).astype(BF16)

        def send_params(d, _):
            param_copy(d).start()
            return 0

        lax.fori_loop(1, NR, send_params, 0)

    def wait_block(b, _):
        @pl.when(b != mine)
        def _():
            pltpu.make_async_remote_copy(
                src_ref=xall.at[b], dst_ref=xall.at[b], send_sem=xs_sem.at[0],
                recv_sem=xr_sem.at[b], device_id={"srow": me}, device_id_type=MESH,
            ).wait_recv()

        return 0

    lax.fori_loop(0, NH * NV, wait_block, 0)

    def x_of(h):
        return xall[h * NV : (h + 1) * NV].reshape(ROWS, NP)

    inside_rows = lax.broadcasted_iota(jnp.int32, (ROWS, WIDE), 1) < NT

    for s in range(NS):
        z = jnp.zeros((ROWS, WIDE), F32)
        for hp in range(PAIRS):
            hs = spans(hp)
            x = jnp.concatenate([x_of(h) for h in hs], axis=1)
            w = jnp.concatenate(
                [kpad[s, LEAD - STEP * h : LEAD - STEP * h + WIDE, :] for h in hs], axis=1
            )
            z = z + lax.dot_general(x, w, (((1,), (1,)), ((), ())), preferred_element_type=F32)
        z = jnp.where(inside_rows, z, 0.0)
        for n in range(NV):
            turned = pltpu.roll(z[n * STEP : (n + 1) * STEP, :], 0, 1, stride=1, stride_axis=0)
            f_ref[s * NV + n : s * NV + n + 1, :] = jnp.sum(turned, axis=0, keepdims=True)

    first = lanes < HALF
    for q in range(NQ):
        low = pltpu.roll(f_ref[:SROWS], (WIDE - PART * q) % WIDE, 1)[:, :NP]
        high = pltpu.roll(f_ref[SROWS:], (WIDE - PART * q + HALF) % WIDE, 1)[:, :NP]
        fsend[q] = jnp.where(first, low, high)

    def sum_copy(d):
        to = lax.rem(grp + d, NQ)
        return pltpu.make_async_remote_copy(
            src_ref=fsend.at[to], dst_ref=frecv.at[d - 1], send_sem=fs_sem.at[d - 1],
            recv_sem=fr_sem.at[d - 1], device_id={"pgrp": to}, device_id_type=MESH,
        )

    for d in range(1, NQ):
        sum_copy(d).start()
    sensor = lax.broadcasted_iota(jnp.int32, (SROWS, NS), 0) // NV
    column = lax.broadcasted_iota(jnp.int32, (SROWS, NS), 1)
    line = noise_ref[...]
    low = jnp.sum(jnp.where(column == sensor, line, 0.0), axis=1, keepdims=True)
    high = jnp.sum(jnp.where(column == sensor + SPLIT, line, 0.0), axis=1, keepdims=True)
    total = fsend[grp] + jnp.where(first, low, high) * pf[:SROWS]
    for d in range(1, NQ):
        sum_copy(d).wait_recv()
        total = total + frecv[d - 1]
    back = pltpu.roll(total, NP - HALF, 1)
    for s in range(NS):
        row = s % SPLIT * NV
        out_ref[s] = (total if s < SPLIT else back)[row : row + NV, :PART]

    for d in range(1, NQ):
        probe_copy(d).wait_send()
        sum_copy(d).wait_send()

    def drain_share(b, _):
        n, h = lax.rem(b, NV), b // NV

        @pl.when(owner_of(h, n) != me)
        def _():
            share_copy(h, n, me).wait_send()

        return 0

    lax.fori_loop(0, NH * NV, drain_share, 0)

    @pl.when(owns)
    def _():
        def drain_params(d, _):
            param_copy(d).wait_send()
            return 0

        lax.fori_loop(1, NR, drain_params, 0)


def on_device(kernel, probes, prior_var, noise_var):
    dma = pltpu.SemaphoreType.DMA
    result = pl.pallas_call(
        kernel_body,
        out_shape=jax.ShapeDtypeStruct((NS, NV, PART), F32),
        in_specs=[pl.BlockSpec(memory_space=pl.ANY)] * 4,
        out_specs=pl.BlockSpec(memory_space=pltpu.VMEM),
        scratch_shapes=[
            pltpu.VMEM((NS, NV, PART), BF16),
            pltpu.VMEM((1, NP), F32),
            pltpu.VMEM((1, NS), F32),
            pltpu.VMEM((NS, TALL, NP), BF16),
            pltpu.VMEM((NS, ROWS, WIDE), BF16),
            pltpu.VMEM((2 * SROWS, WIDE), F32),
            pltpu.VMEM((PROWS, NP), F32),
            pltpu.VMEM((PROWS, NP), BF16),
            pltpu.VMEM((NQ - 1, PROWS, NP), BF16),
            pltpu.VMEM((NH * NV, STEP, NP), F32),
            pltpu.VMEM((NR, STEP, NP), F32),
            pltpu.VMEM((NH * NV, STEP, NP), BF16),
            pltpu.VMEM((2 * SROWS, WIDE), F32),
            pltpu.VMEM((NQ, SROWS, NP), F32),
            pltpu.VMEM((NQ - 1, SROWS, NP), F32),
            dma((4,)),
            dma((NQ - 1,)),
            dma((NQ - 1,)),
            dma((NH * NV,)),
            dma((NR,)),
            dma((NR,)),
            dma((NH * NV,)),
            dma((NQ - 1,)),
            dma((NQ - 1,)),
        ],
        compiler_params=pltpu.CompilerParams(
            collective_id=0, has_side_effects=True, vmem_limit_bytes=60 * 2**20
        ),
        cost_estimate=pl.CostEstimate(flops=2 * 10**9, bytes_accessed=2 * 10**6, transcendentals=0),
    )(probes.transpose(1, 0, 2), prior_var.reshape(1, NP), noise_var.reshape(1, NS), kernel)
    return result.transpose(1, 0, 2)


def solution(mesh):
    placed = (P("srow", None, "pgrp"), P(None, "srow", "pgrp"), P("pgrp"), P("srow"))
    return jax.shard_map(
        on_device, mesh=mesh, in_specs=placed, out_specs=P(None, "srow", "pgrp"), check_vma=False
    )
```

```python
import functools

import jax
import jax.numpy as jnp
from jax import lax
from jax.experimental import pallas as pl
from jax.experimental.pallas import tpu as pltpu
from jax.sharding import PartitionSpec as P

MESH = pl.DeviceIdType.MESH
F32 = jnp.float32
BF16 = jnp.bfloat16

NV, NS, NT, NP = 4, 19, 224, 128
NQ, NR = 4, 32
STEP = 32
NH = NT // STEP
BLOCKS = NH * NV
PAIRS = (NH + 1) // 2
ROWS = NV * STEP
WIDE = 256
LEAD = NT - STEP
TALL = LEAD + WIDE
PART = NT // NQ
HALF = 64
SPLIT = (NS + 1) // 2
SROWS = SPLIT * NV
PROWS = 48


def owner_of(h, n, grp):
    return 8 * n + 2 * lax.rem(n + h // 2 + grp, 4) + lax.rem(h, 2)


def block_of(r, grp):
    n = r // 8
    h = 2 * lax.rem(lax.rem(r // 2, 4) - n - grp + 8, 4) + lax.rem(r, 2)
    return h, n


def kernel_body(
    probes_hbm, prior_hbm, noise_hbm, k_hbm, out_ref,
    probes_ref, prior_ref, noise_ref, kpad, base, y_ref, pf, psend, precv, shares, rsend, rrecv, xall, f_ref,
    fsend, frecv, t_ref,
    in_sem, ps_sem, pr_sem, rs_sem, rr_sem, xs_sem, xr_sem, fs_sem, fr_sem,
):
    me = lax.axis_index("srow")
    grp = lax.axis_index("pgrp")
    my_h, my_n = block_of(me, grp)
    mine = my_h * NV + my_n
    owns = my_h < NH

    barrier = pltpu.get_barrier_semaphore()

    in_copies = [
        pltpu.make_async_copy(src, dst, in_sem.at[i])
        for i, (src, dst) in enumerate(
            (
                (probes_hbm, probes_ref),
                (k_hbm, kpad.at[:, pl.ds(LEAD, NT), :]),
                (prior_hbm, prior_ref),
                (noise_hbm, noise_ref),
            )
        )
    ]
    for copy in in_copies:
        copy.start()

    def greet(d, _):
        pl.semaphore_signal(
            barrier, inc=1, device_id={"srow": lax.rem(me + d, NR)}, device_id_type=MESH
        )
        return 0

    for d in range(1, NQ):
        pl.semaphore_signal(
            barrier, inc=1, device_id={"pgrp": lax.rem(grp + d, NQ)}, device_id_type=MESH
        )
    lax.fori_loop(1, NR, greet, 0)

    pf[...] = jnp.zeros_like(pf)
    in_copies[0].wait()
    for s in range(NS):
        row, lane = s % SPLIT * NV, s // SPLIT * HALF
        pf[row : row + NV, lane : lane + PART] = probes_ref[s].astype(F32)
    psend[...] = pf[...].astype(BF16)

    pl.semaphore_wait(barrier, NQ - 1 + NR - 1)

    def probe_copy(d):
        to = lax.rem(grp + d, NQ)
        return pltpu.make_async_remote_copy(
            src_ref=psend, dst_ref=precv.at[d - 1], send_sem=ps_sem.at[d - 1],
            recv_sem=pr_sem.at[d - 1], device_id={"pgrp": to}, device_id_type=MESH,
        )

    for d in range(1, NQ):
        probe_copy(d).start()
    kpad[:, 0:LEAD, :] = jnp.zeros((NS, LEAD, NP), BF16)
    kpad[:, LEAD + NT : TALL, :] = jnp.zeros((NS, TALL - LEAD - NT, NP), BF16)
    f_ref[...] = jnp.zeros_like(f_ref)
    lanes = lax.broadcasted_iota(jnp.int32, (SROWS, NP), 1)
    zeros = jnp.zeros((SROWS, WIDE - NP), F32)

    def place(part, group):
        part = part[:SROWS].astype(F32)
        for half in range(2):
            lane = half * HALF
            inside = (lanes >= lane) & (lanes < lane + PART)
            wide = jnp.concatenate([jnp.where(inside, part, 0.0), zeros], axis=1)
            shift = lax.rem(group * PART + (WIDE - (STEP - 1) - lane), WIDE)
            y_ref[half * SROWS : (half + 1) * SROWS, :] += pltpu.roll(wide, shift, 1)

    y_ref[...] = jnp.zeros_like(y_ref)
    place(psend, grp)
    for d in range(1, NQ):
        probe_copy(d).wait_recv()
        place(precv[d - 1], lax.rem(grp + NQ - d, NQ))

    inside_wide = lax.broadcasted_iota(jnp.int32, (STEP, WIDE), 1) < NT

    for s in range(NS):
        for n in range(NV):
            line = jnp.broadcast_to(y_ref[s * NV + n : s * NV + n + 1, :], (STEP, WIDE))
            turned = pltpu.roll(line, 0, 1, stride=1, stride_axis=0)
            turned = jnp.where(inside_wide, turned, 0.0)
            base[s, n * STEP : (n + 1) * STEP, :] = turned.astype(BF16)
    in_copies[1].wait()

    def share_copy(h, n, slot):
        return pltpu.make_async_remote_copy(
            src_ref=rsend.at[h * NV + n], dst_ref=rrecv.at[slot], send_sem=rs_sem,
            recv_sem=rr_sem, device_id={"srow": owner_of(h, n, grp)}, device_id_type=MESH,
        )

    def spans(hp):
        return [h for h in (2 * hp, 2 * hp + 1) if h < NH]

    for hp in range(PAIRS):
        hs = spans(hp)

        low = STEP * hs[0] // NP * NP
        x = jnp.concatenate([base[s, :, low:] for s in range(NS)], axis=1)
        w = jnp.concatenate(
            [
                kpad[:, LEAD - STEP * h + low : LEAD - STEP * h + WIDE, :].reshape(-1, NP)
                for h in hs
            ],
            axis=1,
        )
        acc = jnp.dot(x, w, preferred_element_type=F32)
        for j, h in enumerate(hs):
            for n in range(NV):
                share = acc[n * STEP : (n + 1) * STEP, j * NP : (j + 1) * NP]
                shares[h * NV + n] = share
                rsend[h * NV + n] = share.astype(BF16)

        def send_share(j, _):
            j = lax.rem(j + me, NV * len(hs))
            n, h = lax.rem(j, NV), hs[0] + j // NV

            @pl.when(owner_of(h, n, grp) != me)
            def _():
                share_copy(h, n, lax.rem(me - owner_of(h, n, grp) + NR, NR) - 1).start()

            return 0

        lax.fori_loop(0, NV * len(hs), send_share, 0)

    def param_copy(d):
        to = lax.rem(me + d, NR)
        return pltpu.make_async_remote_copy(
            src_ref=xall.at[mine], dst_ref=xall.at[mine], send_sem=xs_sem,
            recv_sem=xr_sem, device_id={"srow": to}, device_id_type=MESH,
        )

    in_copies[2].wait()
    in_copies[3].wait()

    @pl.when(owns)
    def _():
        arrived = rrecv.at[pl.ds(0, NR - 1)]
        pltpu.make_async_copy(arrived, arrived, rr_sem).wait()
        total = shares[mine]
        for slot in range(NR - 1):
            total = total + rrecv[slot].astype(F32)
        scaled = total * prior_ref[...]
        row = lax.broadcasted_iota(jnp.int32, (STEP, STEP), 0)
        col = lax.broadcasted_iota(jnp.int32, (STEP, STEP), 1)
        flip = (row + col == STEP - 1).astype(BF16)
        xall[mine] = jnp.dot(flip, scaled.astype(BF16), preferred_element_type=F32).astype(BF16)

        def send_params(d, _):
            param_copy(d).start()
            return 0

        lax.fori_loop(1, NR, send_params, 0)

    def wait_blocks(ref, sem, count):
        some = ref.at[pl.ds(0, count)]
        pltpu.make_async_copy(some, some, sem).wait()

    @pl.when(owns)
    def _():
        wait_blocks(xall, xr_sem, BLOCKS - 1)
        wait_blocks(rsend, rs_sem, BLOCKS - 1)

    @pl.when(jnp.logical_not(owns))
    def _():
        wait_blocks(xall, xr_sem, BLOCKS)
        wait_blocks(rsend, rs_sem, BLOCKS)

    def x_of(h):
        return xall[h * NV : (h + 1) * NV].reshape(ROWS, NP)

    inside_rows = lax.broadcasted_iota(jnp.int32, (ROWS, WIDE), 1) < NT

    for s in range(NS):
        z = jnp.zeros((ROWS, WIDE), F32)
        for hp in range(PAIRS):
            hs = spans(hp)
            x = jnp.concatenate([x_of(h) for h in hs], axis=1)
            w = jnp.concatenate(
                [kpad[s, LEAD - STEP * h : LEAD - STEP * h + WIDE, :] for h in hs], axis=1
            )
            z = z + lax.dot_general(x, w, (((1,), (1,)), ((), ())), preferred_element_type=F32)
        z = jnp.where(inside_rows, z, 0.0)
        for n in range(NV):
            turned = pltpu.roll(z[n * STEP : (n + 1) * STEP, :], 0, 1, stride=1, stride_axis=0)
            f_ref[s * NV + n : s * NV + n + 1, :] = jnp.sum(turned, axis=0, keepdims=True)

    first = lanes < HALF
    for q in range(NQ):
        low = pltpu.roll(f_ref[:SROWS], (WIDE - PART * q) % WIDE, 1)[:, :NP]
        high = pltpu.roll(f_ref[SROWS:], (WIDE - PART * q + HALF) % WIDE, 1)[:, :NP]
        fsend[q] = jnp.where(first, low, high)

    def sum_copy(d):
        to = lax.rem(grp + d, NQ)
        return pltpu.make_async_remote_copy(
            src_ref=fsend.at[to], dst_ref=frecv.at[d - 1], send_sem=fs_sem.at[d - 1],
            recv_sem=fr_sem.at[d - 1], device_id={"pgrp": to}, device_id_type=MESH,
        )

    for d in range(1, NQ):
        sum_copy(d).start()
    for d in range(1, NQ):
        probe_copy(d).wait_send()

    @pl.when(owns)
    def _():
        all_sent = rrecv.at[pl.ds(0, NR - 1)]
        pltpu.make_async_copy(all_sent, all_sent, xs_sem).wait()

    sensor = lax.broadcasted_iota(jnp.int32, (SROWS, NS), 0) // NV
    column = lax.broadcasted_iota(jnp.int32, (SROWS, NS), 1)
    line = noise_ref[...]
    low = jnp.sum(jnp.where(column == sensor, line, 0.0), axis=1, keepdims=True)
    high = jnp.sum(jnp.where(column == sensor + SPLIT, line, 0.0), axis=1, keepdims=True)
    total = fsend[grp] + jnp.where(first, low, high) * pf[:SROWS]
    for d in range(1, NQ):
        sum_copy(d).wait_recv()
        total = total + frecv[d - 1]
    t_ref[:SROWS] = total
    t_ref[SROWS:] = pltpu.roll(total, NP - HALF, 1)
    for n in range(NV):
        out_ref[n] = t_ref[pl.ds(n, NS, stride=NV), :][:, :PART]
    for d in range(1, NQ):
        sum_copy(d).wait_send()


def on_device(kernel, probes, prior_var, noise_var):
    dma = pltpu.SemaphoreType.DMA
    return pl.pallas_call(
        kernel_body,
        out_shape=jax.ShapeDtypeStruct((NV, NS, PART), F32),
        in_specs=[pl.BlockSpec(memory_space=pl.ANY)] * 4,
        out_specs=pl.BlockSpec(memory_space=pltpu.VMEM),
        scratch_shapes=[
            pltpu.VMEM((NS, NV, PART), BF16),
            pltpu.VMEM((1, NP), F32),
            pltpu.VMEM((1, NS), F32),
            pltpu.VMEM((NS, TALL, NP), BF16),
            pltpu.VMEM((NS, ROWS, WIDE), BF16),
            pltpu.VMEM((2 * SROWS, WIDE), F32),
            pltpu.VMEM((PROWS, NP), F32),
            pltpu.VMEM((PROWS, NP), BF16),
            pltpu.VMEM((NQ - 1, PROWS, NP), BF16),
            pltpu.VMEM((BLOCKS, STEP, NP), F32),
            pltpu.VMEM((BLOCKS, STEP, NP), BF16),
            pltpu.VMEM((NR - 1, STEP, NP), BF16),
            pltpu.VMEM((BLOCKS, STEP, NP), BF16),
            pltpu.VMEM((2 * SROWS, WIDE), F32),
            pltpu.VMEM((NQ, SROWS, NP), F32),
            pltpu.VMEM((NQ - 1, SROWS, NP), F32),
            pltpu.VMEM((2 * SROWS, NP), F32),
            dma((4,)),
            dma((NQ - 1,)),
            dma((NQ - 1,)),
            dma,
            dma,
            dma,
            dma,
            dma((NQ - 1,)),
            dma((NQ - 1,)),
        ],
        compiler_params=pltpu.CompilerParams(
            collective_id=0, has_side_effects=True, vmem_limit_bytes=60 * 2**20
        ),
        cost_estimate=pl.CostEstimate(flops=2 * 10**9, bytes_accessed=2 * 10**6, transcendentals=0),
    )(probes.transpose(1, 0, 2), prior_var.reshape(1, NP), noise_var.reshape(1, NS), kernel)


def solution(mesh):
    placed = (P("srow", None, "pgrp"), P(None, "srow", "pgrp"), P("pgrp"), P("srow"))
    return jax.shard_map(
        on_device, mesh=mesh, in_specs=placed, out_specs=P(None, "srow", "pgrp"), check_vma=False
    )
```

```python
import functools

import jax
import jax.numpy as jnp
from jax import lax
from jax.experimental import pallas as pl
from jax.experimental.pallas import tpu as pltpu
from jax.sharding import PartitionSpec as P

MESH = pl.DeviceIdType.MESH
F32 = jnp.float32
BF16 = jnp.bfloat16

NV, NS, NT, NP = 4, 19, 224, 128
NQ, NR = 4, 32
STEP = 32
NH = NT // STEP
BLOCKS = NH * NV
PAIRS = (NH + 1) // 2
ROWS = NV * STEP
WIDE = 256
LEAD = NT - STEP
TALL = LEAD + WIDE
PART = NT // NQ
HALF = 64
SPLIT = (NS + 1) // 2
SROWS = SPLIT * NV
PROWS = 48


def owner_of(h, n, grp):
    return 8 * n + 2 * lax.rem(n + h // 2 + grp, 4) + h % 2


def block_of(r, grp):
    n = r // 8
    h = 2 * lax.rem(lax.rem(r // 2, 4) - n - grp + 8, 4) + lax.rem(r, 2)
    return h, n


def others_far_first(r):
    x, z, y = r // 8, lax.rem(r // 2, 4), lax.rem(r, 2)
    xs = [8 * lax.rem(x + d, 4) for d in range(4)]
    zs = [2 * lax.rem(z + d, 4) for d in range(4)]
    ys = [y, 1 - y]
    steps = [(dx, dz, dy) for dx in range(4) for dz in range(4) for dy in range(2)]
    steps.sort(key=lambda d: -(min(d[0], 4 - d[0]) + min(d[1], 4 - d[1]) + 2 * d[2]))
    return [xs[dx] + zs[dz] + ys[dy] for dx, dz, dy in steps[:-1]]


def kernel_body(
    probes_hbm, prior_hbm, noise_hbm, k_hbm, out_ref,
    probes_ref, prior_ref, noise_ref, kpad, base, y_ref, pf, psend, precv, shares, rsend, rrecv, xall, f_ref,
    fsend, frecv, t_ref,
    in_sem, ps_sem, pr_sem, rs_sem, rr_sem, xs_sem, xr_sem, fs_sem, fr_sem,
):
    me = lax.axis_index("srow")
    grp = lax.axis_index("pgrp")
    my_h, my_n = block_of(me, grp)
    mine = my_h * NV + my_n
    owns = my_h < NH

    barrier = pltpu.get_barrier_semaphore()

    in_copies = [
        pltpu.make_async_copy(src, dst, in_sem.at[i])
        for i, (src, dst) in enumerate(
            (
                (probes_hbm, probes_ref),
                (k_hbm, kpad.at[:, pl.ds(LEAD, NT), :]),
                (prior_hbm, prior_ref),
                (noise_hbm, noise_ref),
            )
        )
    ]
    far_first = others_far_first(me)
    for to in far_first:
        pl.semaphore_signal(barrier, inc=1, device_id={"srow": to}, device_id_type=MESH)
    for d in range(1, NQ):
        pl.semaphore_signal(
            barrier, inc=1, device_id={"pgrp": lax.rem(grp + d, NQ)}, device_id_type=MESH
        )
    for copy in in_copies:
        copy.start()


    pf[...] = jnp.zeros_like(pf)
    in_copies[0].wait()
    for s in range(NS):
        row, lane = s % SPLIT * NV, s // SPLIT * HALF
        pf[row : row + NV, lane : lane + PART] = probes_ref[s].astype(F32)
    psend[...] = pf[...].astype(BF16)

    pl.semaphore_wait(barrier, NQ - 1 + NR - 1)

    def probe_copy(d):
        to = lax.rem(grp + d, NQ)
        return pltpu.make_async_remote_copy(
            src_ref=psend, dst_ref=precv.at[d - 1], send_sem=ps_sem.at[d - 1],
            recv_sem=pr_sem.at[d - 1], device_id={"pgrp": to}, device_id_type=MESH,
        )

    for d in range(1, NQ):
        probe_copy(d).start()
    kpad[:, 0:LEAD, :] = jnp.zeros((NS, LEAD, NP), BF16)
    kpad[:, LEAD + NT : TALL, :] = jnp.zeros((NS, TALL - LEAD - NT, NP), BF16)
    f_ref[...] = jnp.zeros_like(f_ref)
    lanes = lax.broadcasted_iota(jnp.int32, (SROWS, NP), 1)
    zeros = jnp.zeros((SROWS, WIDE - NP), F32)

    def place(part, group):
        part = part[:SROWS].astype(F32)
        for half in range(2):
            lane = half * HALF
            inside = (lanes >= lane) & (lanes < lane + PART)
            wide = jnp.concatenate([jnp.where(inside, part, 0.0), zeros], axis=1)
            shift = lax.rem(group * PART + (WIDE - (STEP - 1) - lane), WIDE)
            y_ref[half * SROWS : (half + 1) * SROWS, :] += pltpu.roll(wide, shift, 1)

    y_ref[...] = jnp.zeros_like(y_ref)
    place(psend, grp)
    for d in range(1, NQ):
        probe_copy(d).wait_recv()
        place(precv[d - 1], lax.rem(grp + NQ - d, NQ))

    inside_wide = lax.broadcasted_iota(jnp.int32, (STEP, WIDE), 1) < NT

    for s in range(NS):
        for n in range(NV):
            line = jnp.broadcast_to(y_ref[s * NV + n : s * NV + n + 1, :], (STEP, WIDE))
            turned = pltpu.roll(line, 0, 1, stride=1, stride_axis=0)
            turned = jnp.where(inside_wide, turned, 0.0)
            base[s, n * STEP : (n + 1) * STEP, :] = turned.astype(BF16)
    in_copies[1].wait()

    def share_copy(h, n, to):
        slot = lax.rem(me - to + NR, NR) - 1
        return pltpu.make_async_remote_copy(
            src_ref=rsend.at[h * NV + n], dst_ref=rrecv.at[slot], send_sem=rs_sem,
            recv_sem=rr_sem, device_id={"srow": to}, device_id_type=MESH,
        )

    def spans(hp):
        return [h for h in (2 * hp, 2 * hp + 1) if h < NH]

    for hp in range(PAIRS):
        hs = spans(hp)

        low = STEP * hs[0] // NP * NP
        x = jnp.concatenate([base[s, :, low:] for s in range(NS)], axis=1)
        w = jnp.concatenate(
            [
                kpad[:, LEAD - STEP * h + low : LEAD - STEP * h + WIDE, :].reshape(-1, NP)
                for h in hs
            ],
            axis=1,
        )
        acc = jnp.dot(x, w, preferred_element_type=F32)
        for j, h in enumerate(hs):
            for n in range(NV):
                share = acc[n * STEP : (n + 1) * STEP, j * NP : (j + 1) * NP]
                shares[h * NV + n] = share
                rsend[h * NV + n] = share.astype(BF16)

        for j in range(NV * len(hs)):
            h = hs[j // NV]
            n = lax.rem(me // 8 + (2, 1, 3, 0)[j % NV], NV)
            to = owner_of(h, n, grp)

            @pl.when(to != me)
            def _():
                share_copy(h, n, to).start()

    def param_copy(to):
        return pltpu.make_async_remote_copy(
            src_ref=xall.at[mine], dst_ref=xall.at[mine], send_sem=xs_sem,
            recv_sem=xr_sem, device_id={"srow": to}, device_id_type=MESH,
        )

    in_copies[2].wait()
    in_copies[3].wait()

    @pl.when(owns)
    def _():
        arrived = rrecv.at[pl.ds(0, NR - 1)]
        pltpu.make_async_copy(arrived, arrived, rr_sem).wait()
        total = shares[mine]
        for slot in range(NR - 1):
            total = total + rrecv[slot].astype(F32)
        scaled = total * prior_ref[...]
        row = lax.broadcasted_iota(jnp.int32, (STEP, STEP), 0)
        col = lax.broadcasted_iota(jnp.int32, (STEP, STEP), 1)
        flip = (row + col == STEP - 1).astype(BF16)
        xall[mine] = jnp.dot(flip, scaled.astype(BF16), preferred_element_type=F32).astype(BF16)

        for to in far_first:
            param_copy(to).start()

    def wait_blocks(ref, sem, count):
        some = ref.at[pl.ds(0, count)]
        pltpu.make_async_copy(some, some, sem).wait()

    @pl.when(owns)
    def _():
        wait_blocks(xall, xr_sem, BLOCKS - 1)
        wait_blocks(rsend, rs_sem, BLOCKS - 1)

    @pl.when(jnp.logical_not(owns))
    def _():
        wait_blocks(xall, xr_sem, BLOCKS)
        wait_blocks(rsend, rs_sem, BLOCKS)

    def x_of(h):
        return xall[h * NV : (h + 1) * NV].reshape(ROWS, NP)

    inside_rows = lax.broadcasted_iota(jnp.int32, (ROWS, WIDE), 1) < NT

    for s in range(NS):
        z = jnp.zeros((ROWS, WIDE), F32)
        for hp in range(PAIRS):
            hs = spans(hp)
            x = jnp.concatenate([x_of(h) for h in hs], axis=1)
            w = jnp.concatenate(
                [kpad[s, LEAD - STEP * h : LEAD - STEP * h + WIDE, :] for h in hs], axis=1
            )
            z = z + lax.dot_general(x, w, (((1,), (1,)), ((), ())), preferred_element_type=F32)
        z = jnp.where(inside_rows, z, 0.0)
        for n in range(NV):
            turned = pltpu.roll(z[n * STEP : (n + 1) * STEP, :], 0, 1, stride=1, stride_axis=0)
            f_ref[s * NV + n : s * NV + n + 1, :] = jnp.sum(turned, axis=0, keepdims=True)

    first = lanes < HALF
    for q in range(NQ):
        low = pltpu.roll(f_ref[:SROWS], (WIDE - PART * q) % WIDE, 1)[:, :NP]
        high = pltpu.roll(f_ref[SROWS:], (WIDE - PART * q + HALF) % WIDE, 1)[:, :NP]
        fsend[q] = jnp.where(first, low, high)

    def sum_copy(d):
        to = lax.rem(grp + d, NQ)
        return pltpu.make_async_remote_copy(
            src_ref=fsend.at[to], dst_ref=frecv.at[d - 1], send_sem=fs_sem.at[d - 1],
            recv_sem=fr_sem.at[d - 1], device_id={"pgrp": to}, device_id_type=MESH,
        )

    for d in range(1, NQ):
        sum_copy(d).start()
    for d in range(1, NQ):
        probe_copy(d).wait_send()

    @pl.when(owns)
    def _():
        all_sent = rrecv.at[pl.ds(0, NR - 1)]
        pltpu.make_async_copy(all_sent, all_sent, xs_sem).wait()

    sensor = lax.broadcasted_iota(jnp.int32, (SROWS, NS), 0) // NV
    column = lax.broadcasted_iota(jnp.int32, (SROWS, NS), 1)
    line = noise_ref[...]
    low = jnp.sum(jnp.where(column == sensor, line, 0.0), axis=1, keepdims=True)
    high = jnp.sum(jnp.where(column == sensor + SPLIT, line, 0.0), axis=1, keepdims=True)
    total = fsend[grp] + jnp.where(first, low, high) * pf[:SROWS]
    for d in range(1, NQ):
        sum_copy(d).wait_recv()
        total = total + frecv[d - 1]
    t_ref[:SROWS] = total
    t_ref[SROWS:] = pltpu.roll(total, NP - HALF, 1)
    for n in range(NV):
        out_ref[n] = t_ref[pl.ds(n, NS, stride=NV), :][:, :PART]
    for d in range(1, NQ):
        sum_copy(d).wait_send()


def on_device(kernel, probes, prior_var, noise_var):
    dma = pltpu.SemaphoreType.DMA
    arrays = (probes.transpose(1, 0, 2), prior_var.reshape(1, NP), noise_var.reshape(1, NS), kernel)
    return pl.pallas_call(
        kernel_body,
        out_shape=jax.ShapeDtypeStruct((NV, NS, PART), F32),
        in_specs=[pl.BlockSpec(memory_space=pltpu.HBM)] * 4,
        out_specs=pl.BlockSpec(memory_space=pltpu.VMEM),
        scratch_shapes=[
            pltpu.VMEM((NS, NV, PART), BF16),
            pltpu.VMEM((1, NP), F32),
            pltpu.VMEM((1, NS), F32),
            pltpu.VMEM((NS, TALL, NP), BF16),
            pltpu.VMEM((NS, ROWS, WIDE), BF16),
            pltpu.VMEM((2 * SROWS, WIDE), F32),
            pltpu.VMEM((PROWS, NP), F32),
            pltpu.VMEM((PROWS, NP), BF16),
            pltpu.VMEM((NQ - 1, PROWS, NP), BF16),
            pltpu.VMEM((BLOCKS, STEP, NP), F32),
            pltpu.VMEM((BLOCKS, STEP, NP), BF16),
            pltpu.VMEM((NR - 1, STEP, NP), BF16),
            pltpu.VMEM((BLOCKS, STEP, NP), BF16),
            pltpu.VMEM((2 * SROWS, WIDE), F32),
            pltpu.VMEM((NQ, SROWS, NP), F32),
            pltpu.VMEM((NQ - 1, SROWS, NP), F32),
            pltpu.VMEM((2 * SROWS, NP), F32),
            dma((4,)),
            dma((NQ - 1,)),
            dma((NQ - 1,)),
            dma,
            dma,
            dma,
            dma,
            dma((NQ - 1,)),
            dma((NQ - 1,)),
        ],
        compiler_params=pltpu.CompilerParams(
            collective_id=0, has_side_effects=True, vmem_limit_bytes=32 * 2**20
        ),
        cost_estimate=pl.CostEstimate(flops=2 * 10**9, bytes_accessed=2 * 10**6, transcendentals=0),
    )(*(pltpu.with_memory_space_constraint(a, pltpu.HBM) for a in arrays))


def solution(mesh):
    placed = (P("srow", None, "pgrp"), P(None, "srow", "pgrp"), P("pgrp"), P("srow"))
    return jax.shard_map(
        on_device, mesh=mesh, in_specs=placed, out_specs=P(None, "srow", "pgrp"), check_vma=False
    )
```

```python
import functools

import jax
import jax.numpy as jnp
from jax import lax
from jax.experimental import pallas as pl
from jax.experimental.pallas import tpu as pltpu
from jax.sharding import PartitionSpec as P

MESH = pl.DeviceIdType.MESH
F32 = jnp.float32
BF16 = jnp.bfloat16

NV, NS, NT, NP = 4, 19, 224, 128
NQ, NR = 4, 32
STEP = 32
NH = NT // STEP
BLOCKS = NH * NV
PAIRS = (NH + 1) // 2
ROWS = NV * STEP
WIDE = 256
LEAD = NT - STEP
TALL = LEAD + WIDE
PART = NT // NQ
HALF = 64
SPLIT = (NS + 1) // 2
SROWS = SPLIT * NV
PROWS = 48


def owner_of(h, n, grp):
    return 8 * n + 2 * lax.rem(n + h // 2 + grp, 4) + h % 2


def block_of(r, grp):
    n = r // 8
    h = 2 * lax.rem(lax.rem(r // 2, 4) - n - grp + 8, 4) + lax.rem(r, 2)
    return h, n


def others_far_first(r):
    x, z, y = r // 8, lax.rem(r // 2, 4), lax.rem(r, 2)
    xs = [8 * lax.rem(x + d, 4) for d in range(4)]
    zs = [2 * lax.rem(z + d, 4) for d in range(4)]
    ys = [y, 1 - y]
    steps = [(dx, dz, dy) for dx in range(4) for dz in range(4) for dy in range(2)]
    steps.sort(key=lambda d: (-(min(d[0], 4 - d[0]) + min(d[1], 4 - d[1]) + 2 * d[2]), (d[0] * 7 + d[1] * 5 + d[2] * 3) % 11))
    return [xs[dx] + zs[dz] + ys[dy] for dx, dz, dy in steps[:-1]]


def kernel_body(
    probes_hbm, prior_hbm, noise_hbm, k_hbm, out_ref,
    probes_ref, prior_ref, noise_ref, kpad, base, y_ref, pf, psend, precv, shares, rsend, rrecv, xall, f_ref,
    fsend, frecv, t_ref,
    in_sem, ps_sem, pr_sem, rs_sem, rr_sem, xs_sem, xr_sem, fs_sem, fr_sem,
):
    me = lax.axis_index("srow")
    grp = lax.axis_index("pgrp")
    my_h, my_n = block_of(me, grp)
    mine = my_h * NV + my_n
    owns = my_h < NH

    chip, core = grp // 2, lax.rem(grp, 2)

    def mate(d):
        return 2 * (chip if d < 2 else 1 - chip) + (core if d % 2 == 0 else 1 - core)

    barrier = pltpu.get_barrier_semaphore()

    in_copies = [
        pltpu.make_async_copy(src, dst, in_sem.at[i])
        for i, (src, dst) in enumerate(
            (
                (probes_hbm, probes_ref),
                (k_hbm, kpad.at[:, pl.ds(LEAD, NT), :]),
                (prior_hbm, prior_ref),
                (noise_hbm, noise_ref),
            )
        )
    ]
    far_first = others_far_first(me)
    for to in far_first:
        pl.semaphore_signal(barrier, inc=1, device_id={"srow": to}, device_id_type=MESH)
    for d in range(1, NQ):
        pl.semaphore_signal(barrier, inc=1, device_id={"pgrp": mate(d)}, device_id_type=MESH)
    for copy in in_copies:
        copy.start()


    pf[...] = jnp.zeros_like(pf)
    in_copies[0].wait()
    for s in range(NS):
        row, lane = s % SPLIT * NV, s // SPLIT * HALF
        pf[row : row + NV, lane : lane + PART] = probes_ref[s].astype(F32)
    psend[...] = pf[...].astype(BF16)

    pl.semaphore_wait(barrier, NQ - 1 + NR - 1)

    def probe_copy(d):
        return pltpu.make_async_remote_copy(
            src_ref=psend, dst_ref=precv.at[d - 1], send_sem=ps_sem.at[d - 1],
            recv_sem=pr_sem.at[d - 1], device_id={"pgrp": mate(d)}, device_id_type=MESH,
        )

    for d in (3, 2, 1):
        probe_copy(d).start()
    kpad[:, 0:LEAD, :] = jnp.zeros((NS, LEAD, NP), BF16)
    kpad[:, LEAD + NT : TALL, :] = jnp.zeros((NS, TALL - LEAD - NT, NP), BF16)
    f_ref[...] = jnp.zeros_like(f_ref)
    lanes = lax.broadcasted_iota(jnp.int32, (SROWS, NP), 1)
    zeros = jnp.zeros((SROWS, WIDE - NP), F32)

    def place(part, group):
        part = part[:SROWS].astype(F32)
        for half in range(2):
            lane = half * HALF
            inside = (lanes >= lane) & (lanes < lane + PART)
            wide = jnp.concatenate([jnp.where(inside, part, 0.0), zeros], axis=1)
            shift = lax.rem(group * PART + (WIDE - (STEP - 1) - lane), WIDE)
            y_ref[half * SROWS : (half + 1) * SROWS, :] += pltpu.roll(wide, shift, 1)

    y_ref[...] = jnp.zeros_like(y_ref)
    place(psend, grp)
    for d in range(1, NQ):
        probe_copy(d).wait_recv()
        place(precv[d - 1], mate(d))

    inside_wide = lax.broadcasted_iota(jnp.int32, (STEP, WIDE), 1) < NT

    for s in range(NS):
        for n in range(NV):
            line = jnp.broadcast_to(y_ref[s * NV + n : s * NV + n + 1, :], (STEP, WIDE))
            turned = pltpu.roll(line, 0, 1, stride=1, stride_axis=0)
            turned = jnp.where(inside_wide, turned, 0.0)
            base[s, n * STEP : (n + 1) * STEP, :] = turned.astype(BF16)
    in_copies[1].wait()

    def share_copy(block, slot, to):
        return pltpu.make_async_remote_copy(
            src_ref=rsend.at[block], dst_ref=rrecv.at[slot], send_sem=rs_sem,
            recv_sem=rr_sem, device_id={"srow": to}, device_id_type=MESH,
        )

    def spans(hp):
        return [h for h in (2 * hp, 2 * hp + 1) if h < NH]

    for hp in range(PAIRS):
        hs = spans(hp)

        low = STEP * hs[0] // NP * NP
        x = jnp.concatenate([base[s, :, low:] for s in range(NS)], axis=1)
        w = jnp.concatenate(
            [
                kpad[:, LEAD - STEP * h + low : LEAD - STEP * h + WIDE, :].reshape(-1, NP)
                for h in hs
            ],
            axis=1,
        )
        acc = jnp.dot(x, w, preferred_element_type=F32)
        for j, h in enumerate(hs):
            for n in range(NV):
                share = acc[n * STEP : (n + 1) * STEP, j * NP : (j + 1) * NP]
                shares[h * NV + n] = share
                rsend[h * NV + n] = share.astype(BF16)

    for slot, to in enumerate(far_first):
        h, n = block_of(to, grp)

        @pl.when(h < NH)
        def _():
            share_copy(h * NV + n, slot, to).start()

    def param_copy(to):
        return pltpu.make_async_remote_copy(
            src_ref=xall.at[mine], dst_ref=xall.at[mine], send_sem=xs_sem,
            recv_sem=xr_sem, device_id={"srow": to}, device_id_type=MESH,
        )

    in_copies[2].wait()
    in_copies[3].wait()
    first = lanes < HALF
    sensor = lax.broadcasted_iota(jnp.int32, (SROWS, NS), 0) // NV
    column = lax.broadcasted_iota(jnp.int32, (SROWS, NS), 1)
    line = noise_ref[...]
    low = jnp.sum(jnp.where(column == sensor, line, 0.0), axis=1, keepdims=True)
    high = jnp.sum(jnp.where(column == sensor + SPLIT, line, 0.0), axis=1, keepdims=True)
    t_ref[:SROWS] = jnp.where(first, low, high) * pf[:SROWS]

    @pl.when(owns)
    def _():
        arrived = rrecv.at[pl.ds(0, NR - 1)]
        pltpu.make_async_copy(arrived, arrived, rr_sem).wait()
        total = shares[mine]
        for slot in range(NR - 1):
            total = total + rrecv[slot].astype(F32)
        scaled = total * prior_ref[...]
        row = lax.broadcasted_iota(jnp.int32, (STEP, STEP), 0)
        col = lax.broadcasted_iota(jnp.int32, (STEP, STEP), 1)
        flip = (row + col == STEP - 1).astype(BF16)
        xall[mine] = jnp.dot(flip, scaled.astype(BF16), preferred_element_type=F32).astype(BF16)

        for to in far_first:
            param_copy(to).start()

    def wait_blocks(ref, sem, count):
        some = ref.at[pl.ds(0, count)]
        pltpu.make_async_copy(some, some, sem).wait()

    @pl.when(owns)
    def _():
        wait_blocks(xall, xr_sem, BLOCKS - 1)
        wait_blocks(rsend, rs_sem, BLOCKS - 1)

    @pl.when(jnp.logical_not(owns))
    def _():
        wait_blocks(xall, xr_sem, BLOCKS)
        wait_blocks(rsend, rs_sem, BLOCKS)

    def x_of(h):
        return xall[h * NV : (h + 1) * NV].reshape(ROWS, NP)

    inside_rows = lax.broadcasted_iota(jnp.int32, (ROWS, WIDE), 1) < NT

    for s in range(NS):
        z = jnp.zeros((ROWS, WIDE), F32)
        for hp in range(PAIRS):
            hs = spans(hp)
            x = jnp.concatenate([x_of(h) for h in hs], axis=1)
            w = jnp.concatenate(
                [kpad[s, LEAD - STEP * h : LEAD - STEP * h + WIDE, :] for h in hs], axis=1
            )
            z = z + lax.dot_general(x, w, (((1,), (1,)), ((), ())), preferred_element_type=F32)
        z = jnp.where(inside_rows, z, 0.0)
        for n in range(NV):
            turned = pltpu.roll(z[n * STEP : (n + 1) * STEP, :], 0, 1, stride=1, stride_axis=0)
            f_ref[s * NV + n : s * NV + n + 1, :] = jnp.sum(turned, axis=0, keepdims=True)

    def sum_copy(d):
        return pltpu.make_async_remote_copy(
            src_ref=fsend.at[d], dst_ref=frecv.at[d - 1], send_sem=fs_sem.at[d - 1],
            recv_sem=fr_sem.at[d - 1], device_id={"pgrp": mate(d)}, device_id_type=MESH,
        )

    for d in (3, 2, 1, 0):
        shift = WIDE - PART * mate(d)
        low = pltpu.roll(f_ref[:SROWS], lax.rem(shift, WIDE), 1)[:, :NP]
        high = pltpu.roll(f_ref[SROWS:], lax.rem(shift + HALF, WIDE), 1)[:, :NP]
        fsend[d] = jnp.where(first, low, high)
        if d > 0:
            sum_copy(d).start()
    for d in range(1, NQ):
        probe_copy(d).wait_send()

    @pl.when(owns)
    def _():
        all_sent = rrecv.at[pl.ds(0, NR - 1)]
        pltpu.make_async_copy(all_sent, all_sent, xs_sem).wait()

    total = fsend[0] + t_ref[:SROWS]
    for d in range(1, NQ):
        sum_copy(d).wait_recv()
        total = total + frecv[d - 1]
    t_ref[:SROWS] = total
    t_ref[SROWS:] = pltpu.roll(total, NP - HALF, 1)
    for n in range(NV):
        out_ref[n] = t_ref[pl.ds(n, NS, stride=NV), :][:, :PART]
    for d in range(1, NQ):
        sum_copy(d).wait_send()


def on_device(kernel, probes, prior_var, noise_var):
    dma = pltpu.SemaphoreType.DMA
    arrays = (probes.transpose(1, 0, 2), prior_var.reshape(1, NP), noise_var.reshape(1, NS), kernel)
    return pl.pallas_call(
        kernel_body,
        out_shape=jax.ShapeDtypeStruct((NV, NS, PART), F32),
        in_specs=[pl.BlockSpec(memory_space=pltpu.HBM)] * 4,
        out_specs=pl.BlockSpec(memory_space=pltpu.VMEM),
        scratch_shapes=[
            pltpu.VMEM((NS, NV, PART), BF16),
            pltpu.VMEM((1, NP), F32),
            pltpu.VMEM((1, NS), F32),
            pltpu.VMEM((NS, TALL, NP), BF16),
            pltpu.VMEM((NS, ROWS, WIDE), BF16),
            pltpu.VMEM((2 * SROWS, WIDE), F32),
            pltpu.VMEM((PROWS, NP), F32),
            pltpu.VMEM((PROWS, NP), BF16),
            pltpu.VMEM((NQ - 1, PROWS, NP), BF16),
            pltpu.VMEM((BLOCKS, STEP, NP), F32),
            pltpu.VMEM((BLOCKS, STEP, NP), BF16),
            pltpu.VMEM((NR - 1, STEP, NP), BF16),
            pltpu.VMEM((BLOCKS, STEP, NP), BF16),
            pltpu.VMEM((2 * SROWS, WIDE), F32),
            pltpu.VMEM((NQ, SROWS, NP), F32),
            pltpu.VMEM((NQ - 1, SROWS, NP), F32),
            pltpu.VMEM((2 * SROWS, NP), F32),
            dma((4,)),
            dma((NQ - 1,)),
            dma((NQ - 1,)),
            dma,
            dma,
            dma,
            dma,
            dma((NQ - 1,)),
            dma((NQ - 1,)),
        ],
        compiler_params=pltpu.CompilerParams(
            collective_id=0, has_side_effects=True, vmem_limit_bytes=32 * 2**20
        ),
        cost_estimate=pl.CostEstimate(flops=2 * 10**9, bytes_accessed=2 * 10**6, transcendentals=0),
    )(*(pltpu.with_memory_space_constraint(a, pltpu.HBM) for a in arrays))


def solution(mesh):
    placed = (P("srow", None, "pgrp"), P(None, "srow", "pgrp"), P("pgrp"), P("srow"))
    return jax.shard_map(
        on_device, mesh=mesh, in_specs=placed, out_specs=P(None, "srow", "pgrp"), check_vma=False
    )
```

```python
import functools

import jax
import jax.numpy as jnp
from jax import lax
from jax.experimental import pallas as pl
from jax.experimental.pallas import tpu as pltpu
from jax.sharding import PartitionSpec as P

MESH = pl.DeviceIdType.MESH
F32 = jnp.float32
BF16 = jnp.bfloat16

NV, NS, NT, NP = 4, 19, 224, 128
NQ, NR = 4, 32
STEP = 32
NH = NT // STEP
BLOCKS = NH * NV
PAIRS = (NH + 1) // 2
ROWS = NV * STEP
WIDE = 256
LEAD = NT - STEP
TALL = LEAD + WIDE
PART = NT // NQ
HALF = 64
SPLIT = (NS + 1) // 2
SROWS = SPLIT * NV
PROWS = 48


def owner_of(h, n, grp):
    return 8 * n + 2 * lax.rem(n + h // 2 + grp, 4) + h % 2


def block_of(r, grp):
    n = r // 8
    h = 2 * lax.rem(lax.rem(r // 2, 4) - n - grp + 8, 4) + lax.rem(r, 2)
    return h, n


def others_far_first(r):
    x, z, y = r // 8, lax.rem(r // 2, 4), lax.rem(r, 2)
    xs = [8 * lax.rem(x + d, 4) for d in range(4)]
    zs = [2 * lax.rem(z + d, 4) for d in range(4)]
    ys = [y, 1 - y]
    steps = [(dx, dz, dy) for dx in range(4) for dz in range(4) for dy in range(2)]
    steps.sort(key=lambda d: (-(min(d[0], 4 - d[0]) + min(d[1], 4 - d[1]) + 2 * d[2]), (d[0] * 7 + d[1] * 5 + d[2] * 3) % 11))
    return [xs[dx] + zs[dz] + ys[dy] for dx, dz, dy in steps[:-1]]


def kernel_body(
    probes_hbm, prior_hbm, noise_hbm, k_hbm, out_ref,
    probes_ref, prior_ref, noise_ref, kpad, base, y_ref, pf, psend, precv, shares, rsend, rrecv, xall, f_ref,
    fsend, frecv, t_ref,
    in_sem, ps_sem, pr_sem, rs_sem, rr_sem, xs_sem, xr_sem, fs_sem, fr_sem, line_in, plane_in,
):
    me = lax.axis_index("srow")
    grp = lax.axis_index("pgrp")
    my_h, my_n = block_of(me, grp)
    mine = my_h * NV + my_n
    owns = my_h < NH

    chip, core = grp // 2, lax.rem(grp, 2)

    def mate(d):
        return 2 * (chip if d < 2 else 1 - chip) + (core if d % 2 == 0 else 1 - core)

    barrier = pltpu.get_barrier_semaphore()

    in_copies = [
        pltpu.make_async_copy(src, dst, in_sem.at[i])
        for i, (src, dst) in enumerate(
            (
                (probes_hbm, probes_ref),
                (k_hbm, kpad.at[:, pl.ds(LEAD, NT), :]),
                (prior_hbm, prior_ref),
                (noise_hbm, noise_ref),
            )
        )
    ]
    far_first = others_far_first(me)
    x, z, y = me // 8, lax.rem(me // 2, 4), lax.rem(me, 2)
    x_line = [8 * lax.rem(x + d, 4) + 2 * z + y for d in (2, 1, 3)]
    z_line = [8 * x + 2 * lax.rem(z + d, 4) + y for d in (2, 1, 3)]
    y_peer = 8 * x + 2 * z + 1 - y

    def greet(semaphore, to):
        pl.semaphore_signal(semaphore, inc=1, device_id={"srow": to}, device_id_type=MESH)

    for to in [y_peer, *x_line, *z_line]:
        greet(barrier, to)
    for d in range(1, NQ):
        pl.semaphore_signal(barrier, inc=1, device_id={"pgrp": mate(d)}, device_id_type=MESH)
    for copy in in_copies:
        copy.start()


    pf[...] = jnp.zeros_like(pf)
    in_copies[0].wait()
    for s in range(NS):
        row, lane = s % SPLIT * NV, s // SPLIT * HALF
        pf[row : row + NV, lane : lane + PART] = probes_ref[s].astype(F32)
    psend[...] = pf[...].astype(BF16)

    pl.semaphore_wait(barrier, NQ - 1 + 7)

    def probe_copy(d):
        return pltpu.make_async_remote_copy(
            src_ref=psend, dst_ref=precv.at[d - 1], send_sem=ps_sem.at[d - 1],
            recv_sem=pr_sem.at[d - 1], device_id={"pgrp": mate(d)}, device_id_type=MESH,
        )

    for d in (3, 2, 1):
        probe_copy(d).start()
    for to in x_line:
        greet(line_in, to)
    pl.semaphore_wait(line_in, 3)
    greet(plane_in, y_peer)
    kpad[:, 0:LEAD, :] = jnp.zeros((NS, LEAD, NP), BF16)
    kpad[:, LEAD + NT : TALL, :] = jnp.zeros((NS, TALL - LEAD - NT, NP), BF16)
    f_ref[...] = jnp.zeros_like(f_ref)
    lanes = lax.broadcasted_iota(jnp.int32, (SROWS, NP), 1)
    zeros = jnp.zeros((SROWS, WIDE - NP), F32)

    def place(part, group):
        part = part[:SROWS].astype(F32)
        for half in range(2):
            lane = half * HALF
            inside = (lanes >= lane) & (lanes < lane + PART)
            wide = jnp.concatenate([jnp.where(inside, part, 0.0), zeros], axis=1)
            shift = lax.rem(group * PART + (WIDE - (STEP - 1) - lane), WIDE)
            y_ref[half * SROWS : (half + 1) * SROWS, :] += pltpu.roll(wide, shift, 1)

    y_ref[...] = jnp.zeros_like(y_ref)
    place(psend, grp)
    for d in range(1, NQ):
        probe_copy(d).wait_recv()
        place(precv[d - 1], mate(d))

    inside_wide = lax.broadcasted_iota(jnp.int32, (STEP, WIDE), 1) < NT

    for s in range(NS):
        for n in range(NV):
            line = jnp.broadcast_to(y_ref[s * NV + n : s * NV + n + 1, :], (STEP, WIDE))
            turned = pltpu.roll(line, 0, 1, stride=1, stride_axis=0)
            turned = jnp.where(inside_wide, turned, 0.0)
            base[s, n * STEP : (n + 1) * STEP, :] = turned.astype(BF16)
    in_copies[1].wait()

    def share_copy(block, slot, to):
        return pltpu.make_async_remote_copy(
            src_ref=rsend.at[block], dst_ref=rrecv.at[slot], send_sem=rs_sem,
            recv_sem=rr_sem, device_id={"srow": to}, device_id_type=MESH,
        )

    def spans(hp):
        return [h for h in (2 * hp, 2 * hp + 1) if h < NH]

    for hp in range(PAIRS):
        hs = spans(hp)

        low = STEP * hs[0] // NP * NP
        x = jnp.concatenate([base[s, :, low:] for s in range(NS)], axis=1)
        w = jnp.concatenate(
            [
                kpad[:, LEAD - STEP * h + low : LEAD - STEP * h + WIDE, :].reshape(-1, NP)
                for h in hs
            ],
            axis=1,
        )
        acc = jnp.dot(x, w, preferred_element_type=F32)
        for j, h in enumerate(hs):
            for n in range(NV):
                share = acc[n * STEP : (n + 1) * STEP, j * NP : (j + 1) * NP]
                shares[h * NV + n] = share
                rsend[h * NV + n] = share.astype(BF16)

    pl.semaphore_wait(plane_in, 1)
    for slot, to in enumerate(far_first):
        h, n = block_of(to, grp)

        @pl.when(h < NH)
        def _():
            share_copy(h * NV + n, slot, to).start()

    def param_copy(to):
        return pltpu.make_async_remote_copy(
            src_ref=xall.at[mine], dst_ref=xall.at[mine], send_sem=xs_sem,
            recv_sem=xr_sem, device_id={"srow": to}, device_id_type=MESH,
        )

    in_copies[2].wait()
    in_copies[3].wait()
    first = lanes < HALF
    sensor = lax.broadcasted_iota(jnp.int32, (SROWS, NS), 0) // NV
    column = lax.broadcasted_iota(jnp.int32, (SROWS, NS), 1)
    line = noise_ref[...]
    low = jnp.sum(jnp.where(column == sensor, line, 0.0), axis=1, keepdims=True)
    high = jnp.sum(jnp.where(column == sensor + SPLIT, line, 0.0), axis=1, keepdims=True)
    t_ref[:SROWS] = jnp.where(first, low, high) * pf[:SROWS]

    @pl.when(owns)
    def _():
        arrived = rrecv.at[pl.ds(0, NR - 1)]
        pltpu.make_async_copy(arrived, arrived, rr_sem).wait()
        total = shares[mine]
        for slot in range(NR - 1):
            total = total + rrecv[slot].astype(F32)
        scaled = total * prior_ref[...]
        row = lax.broadcasted_iota(jnp.int32, (STEP, STEP), 0)
        col = lax.broadcasted_iota(jnp.int32, (STEP, STEP), 1)
        flip = (row + col == STEP - 1).astype(BF16)
        xall[mine] = jnp.dot(flip, scaled.astype(BF16), preferred_element_type=F32).astype(BF16)

        for to in far_first:
            param_copy(to).start()

    def wait_blocks(ref, sem, count):
        some = ref.at[pl.ds(0, count)]
        pltpu.make_async_copy(some, some, sem).wait()

    @pl.when(owns)
    def _():
        wait_blocks(xall, xr_sem, BLOCKS - 1)
        wait_blocks(rsend, rs_sem, BLOCKS - 1)

    @pl.when(jnp.logical_not(owns))
    def _():
        wait_blocks(xall, xr_sem, BLOCKS)
        wait_blocks(rsend, rs_sem, BLOCKS)

    def x_of(h):
        return xall[h * NV : (h + 1) * NV].reshape(ROWS, NP)

    inside_rows = lax.broadcasted_iota(jnp.int32, (ROWS, WIDE), 1) < NT

    for s in range(NS):
        z = jnp.zeros((ROWS, WIDE), F32)
        for hp in range(PAIRS):
            hs = spans(hp)
            x = jnp.concatenate([x_of(h) for h in hs], axis=1)
            w = jnp.concatenate(
                [kpad[s, LEAD - STEP * h : LEAD - STEP * h + WIDE, :] for h in hs], axis=1
            )
            z = z + lax.dot_general(x, w, (((1,), (1,)), ((), ())), preferred_element_type=F32)
        z = jnp.where(inside_rows, z, 0.0)
        for n in range(NV):
            turned = pltpu.roll(z[n * STEP : (n + 1) * STEP, :], 0, 1, stride=1, stride_axis=0)
            f_ref[s * NV + n : s * NV + n + 1, :] = jnp.sum(turned, axis=0, keepdims=True)

    def sum_copy(d):
        return pltpu.make_async_remote_copy(
            src_ref=fsend.at[d], dst_ref=frecv.at[d - 1], send_sem=fs_sem.at[d - 1],
            recv_sem=fr_sem.at[d - 1], device_id={"pgrp": mate(d)}, device_id_type=MESH,
        )

    for d in (3, 2, 1, 0):
        shift = WIDE - PART * mate(d)
        low = pltpu.roll(f_ref[:SROWS], lax.rem(shift, WIDE), 1)[:, :NP]
        high = pltpu.roll(f_ref[SROWS:], lax.rem(shift + HALF, WIDE), 1)[:, :NP]
        fsend[d] = jnp.where(first, low, high)
        if d > 0:
            sum_copy(d).start()
    for d in range(1, NQ):
        probe_copy(d).wait_send()

    @pl.when(owns)
    def _():
        all_sent = rrecv.at[pl.ds(0, NR - 1)]
        pltpu.make_async_copy(all_sent, all_sent, xs_sem).wait()

    total = fsend[0] + t_ref[:SROWS]
    for d in range(1, NQ):
        sum_copy(d).wait_recv()
        total = total + frecv[d - 1]
    t_ref[:SROWS] = total
    t_ref[SROWS:] = pltpu.roll(total, NP - HALF, 1)
    for n in range(NV):
        out_ref[n] = t_ref[pl.ds(n, NS, stride=NV), :][:, :PART]
    for d in range(1, NQ):
        sum_copy(d).wait_send()


def on_device(kernel, probes, prior_var, noise_var):
    dma = pltpu.SemaphoreType.DMA
    arrays = (probes.transpose(1, 0, 2), prior_var.reshape(1, NP), noise_var.reshape(1, NS), kernel)
    return pl.pallas_call(
        kernel_body,
        out_shape=jax.ShapeDtypeStruct((NV, NS, PART), F32),
        in_specs=[pl.BlockSpec(memory_space=pltpu.HBM)] * 4,
        out_specs=pl.BlockSpec(memory_space=pltpu.VMEM),
        scratch_shapes=[
            pltpu.VMEM((NS, NV, PART), BF16),
            pltpu.VMEM((1, NP), F32),
            pltpu.VMEM((1, NS), F32),
            pltpu.VMEM((NS, TALL, NP), BF16),
            pltpu.VMEM((NS, ROWS, WIDE), BF16),
            pltpu.VMEM((2 * SROWS, WIDE), F32),
            pltpu.VMEM((PROWS, NP), F32),
            pltpu.VMEM((PROWS, NP), BF16),
            pltpu.VMEM((NQ - 1, PROWS, NP), BF16),
            pltpu.VMEM((BLOCKS, STEP, NP), F32),
            pltpu.VMEM((BLOCKS, STEP, NP), BF16),
            pltpu.VMEM((NR - 1, STEP, NP), BF16),
            pltpu.VMEM((BLOCKS, STEP, NP), BF16),
            pltpu.VMEM((2 * SROWS, WIDE), F32),
            pltpu.VMEM((NQ, SROWS, NP), F32),
            pltpu.VMEM((NQ - 1, SROWS, NP), F32),
            pltpu.VMEM((2 * SROWS, NP), F32),
            dma((4,)),
            dma((NQ - 1,)),
            dma((NQ - 1,)),
            dma,
            dma,
            dma,
            dma,
            dma((NQ - 1,)),
            dma((NQ - 1,)),
            pltpu.SemaphoreType.REGULAR,
            pltpu.SemaphoreType.REGULAR,
        ],
        compiler_params=pltpu.CompilerParams(
            collective_id=0, has_side_effects=True, vmem_limit_bytes=32 * 2**20
        ),
        cost_estimate=pl.CostEstimate(flops=2 * 10**9, bytes_accessed=2 * 10**6, transcendentals=0),
    )(*(pltpu.with_memory_space_constraint(a, pltpu.HBM) for a in arrays))


def solution(mesh):
    placed = (P("srow", None, "pgrp"), P(None, "srow", "pgrp"), P("pgrp"), P("srow"))
    return jax.shard_map(
        on_device, mesh=mesh, in_specs=placed, out_specs=P(None, "srow", "pgrp"), check_vma=False
    )
```

```python
import functools

import jax
import jax.numpy as jnp
from jax import lax
from jax.experimental import pallas as pl
from jax.experimental.pallas import tpu as pltpu
from jax.sharding import PartitionSpec as P

MESH = pl.DeviceIdType.MESH
F32 = jnp.float32
BF16 = jnp.bfloat16

NV, NS, NT, NP = 4, 19, 224, 128
NQ, NR = 4, 32
ROOT = NR - 1
STEP = 32
NH = NT // STEP
BLOCKS = NH * NV
PAIRS = (NH + 1) // 2
ROWS = NV * STEP
WIDE = 256
LEAD = NT - STEP
TALL = LEAD + WIDE
PART = NT // NQ
HALF = 64
SPLIT = (NS + 1) // 2
SROWS = SPLIT * NV
PROWS = 48


def owner_of(h, n, grp):
    return 8 * n + 2 * lax.rem(n + h // 2 + grp, 4) + h % 2


def block_of(r, grp):
    n = r // 8
    h = 2 * lax.rem(lax.rem(r // 2, 4) - n - grp + 8, 4) + lax.rem(r, 2)
    return h, n


def others_far_first(r):
    x, z, y = r // 8, lax.rem(r // 2, 4), lax.rem(r, 2)
    xs = [8 * lax.rem(x + d, 4) for d in range(4)]
    zs = [2 * lax.rem(z + d, 4) for d in range(4)]
    ys = [y, 1 - y]
    steps = [(dx, dz, dy) for dx in range(4) for dz in range(4) for dy in range(2)]
    steps.sort(key=lambda d: (-(min(d[0], 4 - d[0]) + min(d[1], 4 - d[1]) + 2 * d[2]), (d[0] * 7 + d[1] * 5 + d[2] * 3) % 11))
    return [xs[dx] + zs[dz] + ys[dy] for dx, dz, dy in steps[:-1]]


def kernel_body(
    probes_hbm, prior_hbm, noise_hbm, k_hbm, out_ref,
    probes_ref, prior_ref, noise_ref, kpad, base, y_ref, pf, psend, precv, shares, rsend, rrecv, xall, f_ref,
    fsend, frecv, t_ref,
    in_sem, ps_sem, pr_sem, rs_sem, rr_sem, xs_sem, xr_sem, fs_sem, fr_sem, all_in,
):
    me = lax.axis_index("srow")
    grp = lax.axis_index("pgrp")
    my_h, my_n = block_of(me, grp)
    mine = my_h * NV + my_n
    owns = my_h < NH

    chip, core = grp // 2, lax.rem(grp, 2)

    def mate(d):
        return 2 * (chip if d < 2 else 1 - chip) + (core if d % 2 == 0 else 1 - core)

    barrier = pltpu.get_barrier_semaphore()

    in_copies = [
        pltpu.make_async_copy(src, dst, in_sem.at[i])
        for i, (src, dst) in enumerate(
            (
                (probes_hbm, probes_ref),
                (k_hbm, kpad.at[:, pl.ds(LEAD, NT), :]),
                (prior_hbm, prior_ref),
                (noise_hbm, noise_ref),
            )
        )
    ]
    far_first = others_far_first(me)
    for d in range(1, NQ):
        pl.semaphore_signal(barrier, inc=1, device_id={"pgrp": mate(d)}, device_id_type=MESH)

    @pl.when(me != ROOT)
    def _():
        pl.semaphore_signal(barrier, inc=1, device_id={"srow": ROOT}, device_id_type=MESH)

    for copy in in_copies:
        copy.start()


    pf[...] = jnp.zeros_like(pf)
    in_copies[0].wait()
    for s in range(NS):
        row, lane = s % SPLIT * NV, s // SPLIT * HALF
        pf[row : row + NV, lane : lane + PART] = probes_ref[s].astype(F32)
    psend[...] = pf[...].astype(BF16)

    pl.semaphore_wait(barrier, NQ - 1 + (NR - 1) * (me // ROOT))

    def probe_copy(d):
        return pltpu.make_async_remote_copy(
            src_ref=psend, dst_ref=precv.at[d - 1], send_sem=ps_sem.at[d - 1],
            recv_sem=pr_sem.at[d - 1], device_id={"pgrp": mate(d)}, device_id_type=MESH,
        )

    for d in (3, 2, 1):
        probe_copy(d).start()

    @pl.when(me == ROOT)
    def _():
        for to in far_first:
            pl.semaphore_signal(all_in, inc=1, device_id={"srow": to}, device_id_type=MESH)

    kpad[:, 0:LEAD, :] = jnp.zeros((NS, LEAD, NP), BF16)
    kpad[:, LEAD + NT : TALL, :] = jnp.zeros((NS, TALL - LEAD - NT, NP), BF16)
    f_ref[...] = jnp.zeros_like(f_ref)
    lanes = lax.broadcasted_iota(jnp.int32, (SROWS, NP), 1)
    zeros = jnp.zeros((SROWS, WIDE - NP), F32)

    def place(part, group):
        part = part[:SROWS].astype(F32)
        for half in range(2):
            lane = half * HALF
            inside = (lanes >= lane) & (lanes < lane + PART)
            wide = jnp.concatenate([jnp.where(inside, part, 0.0), zeros], axis=1)
            shift = lax.rem(group * PART + (WIDE - (STEP - 1) - lane), WIDE)
            y_ref[half * SROWS : (half + 1) * SROWS, :] += pltpu.roll(wide, shift, 1)

    y_ref[...] = jnp.zeros_like(y_ref)
    place(psend, grp)
    for d in range(1, NQ):
        probe_copy(d).wait_recv()
        place(precv[d - 1], mate(d))

    inside_wide = lax.broadcasted_iota(jnp.int32, (STEP, WIDE), 1) < NT

    for s in range(NS):
        for n in range(NV):
            line = jnp.broadcast_to(y_ref[s * NV + n : s * NV + n + 1, :], (STEP, WIDE))
            turned = pltpu.roll(line, 0, 1, stride=1, stride_axis=0)
            turned = jnp.where(inside_wide, turned, 0.0)
            base[s, n * STEP : (n + 1) * STEP, :] = turned.astype(BF16)
    in_copies[1].wait()

    def share_copy(block, slot, to):
        return pltpu.make_async_remote_copy(
            src_ref=rsend.at[block], dst_ref=rrecv.at[slot], send_sem=rs_sem,
            recv_sem=rr_sem, device_id={"srow": to}, device_id_type=MESH,
        )

    def spans(hp):
        return [h for h in (2 * hp, 2 * hp + 1) if h < NH]

    for hp in range(PAIRS):
        hs = spans(hp)

        low = STEP * hs[0] // NP * NP
        x = jnp.concatenate([base[s, :, low:] for s in range(NS)], axis=1)
        w = jnp.concatenate(
            [
                kpad[:, LEAD - STEP * h + low : LEAD - STEP * h + WIDE, :].reshape(-1, NP)
                for h in hs
            ],
            axis=1,
        )
        acc = jnp.dot(x, w, preferred_element_type=F32)
        for j, h in enumerate(hs):
            for n in range(NV):
                share = acc[n * STEP : (n + 1) * STEP, j * NP : (j + 1) * NP]
                shares[h * NV + n] = share
                rsend[h * NV + n] = share.astype(BF16)

    @pl.when(me != ROOT)
    def _():
        pl.semaphore_wait(all_in, 1)

    for slot, to in enumerate(far_first):
        h, n = block_of(to, grp)

        @pl.when(h < NH)
        def _():
            share_copy(h * NV + n, slot, to).start()

    def param_copy(to):
        return pltpu.make_async_remote_copy(
            src_ref=xall.at[mine], dst_ref=xall.at[mine], send_sem=xs_sem,
            recv_sem=xr_sem, device_id={"srow": to}, device_id_type=MESH,
        )

    in_copies[2].wait()
    in_copies[3].wait()
    first = lanes < HALF
    sensor = lax.broadcasted_iota(jnp.int32, (SROWS, NS), 0) // NV
    column = lax.broadcasted_iota(jnp.int32, (SROWS, NS), 1)
    line = noise_ref[...]
    low = jnp.sum(jnp.where(column == sensor, line, 0.0), axis=1, keepdims=True)
    high = jnp.sum(jnp.where(column == sensor + SPLIT, line, 0.0), axis=1, keepdims=True)
    t_ref[:SROWS] = jnp.where(first, low, high) * pf[:SROWS]

    @pl.when(owns)
    def _():
        arrived = rrecv.at[pl.ds(0, NR - 1)]
        pltpu.make_async_copy(arrived, arrived, rr_sem).wait()
        total = shares[mine]
        for slot in range(NR - 1):
            total = total + rrecv[slot].astype(F32)
        scaled = total * prior_ref[...]
        row = lax.broadcasted_iota(jnp.int32, (STEP, STEP), 0)
        col = lax.broadcasted_iota(jnp.int32, (STEP, STEP), 1)
        flip = (row + col == STEP - 1).astype(BF16)
        xall[mine] = jnp.dot(flip, scaled.astype(BF16), preferred_element_type=F32).astype(BF16)

        for to in far_first:
            param_copy(to).start()

    def wait_blocks(ref, sem, count):
        some = ref.at[pl.ds(0, count)]
        pltpu.make_async_copy(some, some, sem).wait()

    @pl.when(owns)
    def _():
        wait_blocks(xall, xr_sem, BLOCKS - 1)
        wait_blocks(rsend, rs_sem, BLOCKS - 1)

    @pl.when(jnp.logical_not(owns))
    def _():
        wait_blocks(xall, xr_sem, BLOCKS)
        wait_blocks(rsend, rs_sem, BLOCKS)

    def x_of(h):
        return xall[h * NV : (h + 1) * NV].reshape(ROWS, NP)

    inside_rows = lax.broadcasted_iota(jnp.int32, (ROWS, WIDE), 1) < NT

    upper = lax.broadcasted_iota(jnp.int32, (ROWS, NP), 1) < NT - NP
    x_all = jnp.concatenate([x_of(h) for h in range(NH)], axis=1)
    few = NP // STEP

    def halves_of(sensors, at, count):
        w = jnp.concatenate(
            [
                jnp.concatenate(
                    [kpad[s, LEAD - STEP * h + at : LEAD - STEP * h + at + NP, :] for h in range(count)],
                    axis=1,
                )
                for s in sensors
            ],
            axis=0,
        )
        return lax.dot_general(
            x_all[:, : count * NP], w, (((1,), (1,)), ((), ())), preferred_element_type=F32
        )

    def forward_sensors(sensors):
        low = halves_of(sensors, 0, few)
        high = halves_of(sensors, NP, NH)
        for i, s in enumerate(sensors):
            lane = slice(i * NP, (i + 1) * NP)
            z = jnp.concatenate([low[:, lane], jnp.where(upper, high[:, lane], 0.0)], axis=1)
            for n in range(NV):
                turned = pltpu.roll(z[n * STEP : (n + 1) * STEP, :], 0, 1, stride=1, stride_axis=0)
                f_ref[s * NV + n : s * NV + n + 1, :] = jnp.sum(turned, axis=0, keepdims=True)

    for s in range(0, NS, 2):
        forward_sensors(range(s, min(s + 2, NS)))

    def sum_copy(d):
        return pltpu.make_async_remote_copy(
            src_ref=fsend.at[d], dst_ref=frecv.at[d - 1], send_sem=fs_sem.at[d - 1],
            recv_sem=fr_sem.at[d - 1], device_id={"pgrp": mate(d)}, device_id_type=MESH,
        )

    for d in (3, 2, 1, 0):
        shift = WIDE - PART * mate(d)
        low = pltpu.roll(f_ref[:SROWS], lax.rem(shift, WIDE), 1)[:, :NP]
        high = pltpu.roll(f_ref[SROWS:], lax.rem(shift + HALF, WIDE), 1)[:, :NP]
        fsend[d] = jnp.where(first, low, high)
        if d > 0:
            sum_copy(d).start()
    for d in range(1, NQ):
        probe_copy(d).wait_send()

    @pl.when(owns)
    def _():
        all_sent = rrecv.at[pl.ds(0, NR - 1)]
        pltpu.make_async_copy(all_sent, all_sent, xs_sem).wait()

    total = fsend[0] + t_ref[:SROWS]
    for d in range(1, NQ):
        sum_copy(d).wait_recv()
        total = total + frecv[d - 1]
    t_ref[:SROWS] = total
    t_ref[SROWS:] = pltpu.roll(total, NP - HALF, 1)
    for n in range(NV):
        out_ref[n] = t_ref[pl.ds(n, NS, stride=NV), :][:, :PART]
    for d in range(1, NQ):
        sum_copy(d).wait_send()


def on_device(kernel, probes, prior_var, noise_var):
    dma = pltpu.SemaphoreType.DMA
    arrays = (probes.transpose(1, 0, 2), prior_var.reshape(1, NP), noise_var.reshape(1, NS), kernel)
    return pl.pallas_call(
        kernel_body,
        out_shape=jax.ShapeDtypeStruct((NV, NS, PART), F32),
        in_specs=[pl.BlockSpec(memory_space=pltpu.HBM)] * 4,
        out_specs=pl.BlockSpec(memory_space=pltpu.VMEM),
        scratch_shapes=[
            pltpu.VMEM((NS, NV, PART), BF16),
            pltpu.VMEM((1, NP), F32),
            pltpu.VMEM((1, NS), F32),
            pltpu.VMEM((NS, TALL, NP), BF16),
            pltpu.VMEM((NS, ROWS, WIDE), BF16),
            pltpu.VMEM((2 * SROWS, WIDE), F32),
            pltpu.VMEM((PROWS, NP), F32),
            pltpu.VMEM((PROWS, NP), BF16),
            pltpu.VMEM((NQ - 1, PROWS, NP), BF16),
            pltpu.VMEM((BLOCKS, STEP, NP), F32),
            pltpu.VMEM((BLOCKS, STEP, NP), BF16),
            pltpu.VMEM((NR - 1, STEP, NP), BF16),
            pltpu.VMEM((BLOCKS, STEP, NP), BF16),
            pltpu.VMEM((2 * SROWS, WIDE), F32),
            pltpu.VMEM((NQ, SROWS, NP), F32),
            pltpu.VMEM((NQ - 1, SROWS, NP), F32),
            pltpu.VMEM((2 * SROWS, NP), F32),
            dma((4,)),
            dma((NQ - 1,)),
            dma((NQ - 1,)),
            dma,
            dma,
            dma,
            dma,
            dma((NQ - 1,)),
            dma((NQ - 1,)),
            pltpu.SemaphoreType.REGULAR,
        ],
        compiler_params=pltpu.CompilerParams(
            collective_id=0, has_side_effects=True, vmem_limit_bytes=32 * 2**20
        ),
        cost_estimate=pl.CostEstimate(flops=2 * 10**9, bytes_accessed=2 * 10**6, transcendentals=0),
    )(*(pltpu.with_memory_space_constraint(a, pltpu.HBM) for a in arrays))


def solution(mesh):
    placed = (P("srow", None, "pgrp"), P(None, "srow", "pgrp"), P("pgrp"), P("srow"))
    return jax.shard_map(
        on_device, mesh=mesh, in_specs=placed, out_specs=P(None, "srow", "pgrp"), check_vma=False
    )
```
